32 devices in a mesh: parts: 2 (over x), blk: 16 (over z, y, core).
Axes of the slice: x: 2, y: 2, z: 4, core: 2. Of those that a mesh axis runs over, the one named last changes fastest.
Arguments:
- activations: bfloat16 [32, 160, 4096], P(('parts', 'blk')), parts along dimension 0, may hold values from -6 to 6
- output_grads: bfloat16 [32, 160, 14336], P(('parts', 'blk')), parts along dimension 0, may hold values from -6 to 6
- basis_in: bfloat16 [4096, 4096], P('blk'), may hold values from -0.09375 to 0.09375
- basis_out: bfloat16 [14336, 14336], P('blk'), may hold values from -0.046875 to 0.046875
- query_left: bfloat16 [16, 32, 4096], P('blk'), may hold values from -0.09375 to 0.09375
- query_right: bfloat16 [16, 32, 14336], P('blk'), may hold values from -0.046875 to 0.046875
- owners: int32 [4], replicated, may hold values from 0 to 15, as said below
- lengths: int32 [32], P('parts'), parts along dimension 0, may hold values from 1 to 160, 1920 in all
- slot_plan: int32 [32], P('parts'), parts along dimension 0, may hold values from 0 to 15, each once
Outputs:
- scores: float32 [32, 4], P(('parts', 'blk')), parts along dimension 0
The draws below stay inside these ranges and needn't reach their ends.
There are 2 independent parts, one for each index of `parts`. The reference program is written for one: setup_inputs(seed, part) draws one part's arguments, and reference() takes and returns one part's arrays. A program takes and returns all parts, laid end to end along the dimension named above; an argument that names none is the same for every part. Nothing has to cross between parts.
Inputs may be any that keep to these rules, and one draw needn't show every extreme that they name: `owners`: distinct slots of blk.
All inputs are finite; a program needn't handle non-finite values.
Results may differ from the reference program's by a relative error of at most 0.01.
Values may be sent and summed in bfloat16 or wider, within the bound.
No kernel may reach another device: no remote copies, remote signals or barrier semaphores. Data moves between devices by JAX's collectives and lax.ppermute only.
A program may use at most 128 MiB of HBM per device.

```python
import math
import jax
import jax.numpy as jnp
import numpy as np
from jax import lax

D = 4096
FF = 14336
FW = 14336
R = 32
QUERIES = 4
LMAX = 160
SEQS = 16
TOKENS = 2560
N_BLK = 16


def draw_owners(key, part):
    return jax.random.permutation(key, N_BLK)[:QUERIES].astype(jnp.int32)


def block_scale(rng, dims, cuts, low, high):
    def one(dim, parts):
        draws = jax.random.uniform(jax.random.fold_in(jax.random.fold_in(rng, 6), dim), (parts,), jnp.float32, low / len(cuts), high / len(cuts))
        return jnp.repeat(jnp.exp(draws), dims[dim] // parts).reshape((-1,) + (1,) * (len(dims) - dim - 1))

    level = one(*cuts[0])
    for cut in cuts[1:]:
        level = level * one(*cut)
    return level


def profile(count, total, bound, skew):
    loads = [(1 << 20) // math.isqrt(rank ** skew) + 1 for rank in range(2, count + 1)]
    rest, holding = total - bound - (count - 1), [1] * (count - 1)
    while rest > 0:
        free = [i for i in range(count - 1) if holding[i] < bound]
        mass, left = sum([loads[i] for i in free]), rest
        for i in free:
            addition = min(bound - holding[i], max(1, left * loads[i] // mass), rest)
            holding[i] = holding[i] + addition
            rest = rest - addition
    return np.array([bound] + holding)


def ragged_sizes(own_key, number_of, total, limit, slope):
    if number_of == 2:
        one = jax.random.randint(own_key, (), max(1, total - limit), min(limit, total - 1) + 1)
        return jnp.stack([one, total - one])
    sizes = jnp.asarray(profile(number_of, total, limit, slope), jnp.int32)
    twos = (number_of - 1) // 2
    giver, sink = sizes[1:1 + 2 * twos:2], sizes[2:2 + 2 * twos:2]
    room = jnp.minimum(giver - 1, limit - sink)
    passed = jax.random.randint(jax.random.fold_in(own_key, 1), (twos,), 0, 1 << 20) % (room + 1)
    sizes = sizes.at[1:1 + 2 * twos:2].set(giver - passed).at[2:2 + 2 * twos:2].set(sink + passed)
    return sizes[jax.random.permutation(jax.random.fold_in(own_key, 2), number_of)]


def centred(stream_key, shape, spread, bound, shards=(), kind=jnp.bfloat16):
    factor_of = block_scale(stream_key, shape, shards, -0.22, 0.18) if shards else 1.0
    values = jax.random.normal(stream_key, shape, jnp.float32) * spread * factor_of
    return jnp.minimum(jnp.maximum(values, -bound), bound).astype(kind)


def setup_inputs(seed: int = 0, part: int = 0) -> dict:
    splits = jax.random.split(jax.random.key(seed), 10)
    part_keys = jax.random.split(jax.random.fold_in(splits[9], part), 10)
    return {
        "activations": centred(part_keys[0], (SEQS, LMAX, D), 1.0, 6.0, ((0, 16),)),
        "output_grads": centred(part_keys[1], (SEQS, LMAX, FF), 1.0, 6.0, ((0, 16),)),
        "basis_in": centred(splits[2], (D, D), D ** -0.5, 0.09375, ((0, 16),)),
        "basis_out": centred(splits[3], (FF, FW), FF ** -0.5, 0.046875, ((0, 16),)),
        "query_left": centred(splits[4], (N_BLK, R, D), D ** -0.5, 0.09375, ((0, 16),)),
        "query_right": centred(splits[5], (N_BLK, R, FW), FW ** -0.5, 0.046875, ((0, 16),)),
        "owners": draw_owners(jax.random.fold_in(splits[9], 71), part),
        "lengths": ragged_sizes(part_keys[7], SEQS, SEQS * LMAX * 3 // 4, LMAX, 2).astype(jnp.int32),
        "slot_plan": jax.random.permutation(part_keys[8], SEQS).astype(jnp.int32),
    }


def reference(activations, output_grads, basis_in, basis_out, query_left, query_right, owners, lengths, slot_plan):
    left = query_left[owners].reshape(QUERIES * R, D)
    right = query_right[owners].reshape(QUERIES * R, FW)
    contract = (((1,), (1,)), ((), ()))
    rotated_in = lax.dot_general(basis_in, left, contract, preferred_element_type=jnp.float32).astype(jnp.bfloat16)
    rotated_out = lax.dot_general(basis_out, right, contract, preferred_element_type=jnp.float32).astype(jnp.bfloat16)
    project_in = jnp.dot(activations.reshape(TOKENS, D), rotated_in, preferred_element_type=jnp.float32)
    project_out = jnp.dot(output_grads.reshape(TOKENS, FF), rotated_out, preferred_element_type=jnp.float32)
    products = (project_in * project_out).reshape(SEQS, LMAX, QUERIES, R)
    slot_lengths = lengths[slot_plan]
    live_mask = (jnp.arange(LMAX)[None, :] < slot_lengths[:, None]).astype(jnp.float32)
    slot_score = jnp.einsum('stqr,st->sq', products, live_mask) / R
    return jnp.zeros((SEQS, QUERIES), jnp.float32).at[slot_plan].set(slot_score)
```

```python
import functools

import jax
import jax.numpy as jnp
from jax import lax
from jax.experimental import pallas as pl
from jax.experimental.pallas import tpu as pltpu
from jax.sharding import PartitionSpec as P

ROWS = (((1,), (1,)), ((), ()))


def rotate_kernel(part, own_at, sib_at, own, sib, basis_in, basis_out, out, acc):
    step = pl.program_id(0)
    wide_in = basis_in.shape[1]
    rows_in = basis_in.shape[0]

    @pl.when(step == 0)
    def _():
        acc[...] = jnp.zeros_like(acc)

    left = jnp.concatenate([own[0, :, :wide_in], sib[0, :, :wide_in]], axis=0)
    right = jnp.concatenate([own[0, :, wide_in:], sib[0, :, wide_in:]], axis=0)
    acc[:, :rows_in] += lax.dot_general(
        left, basis_in[...], ROWS, preferred_element_type=jnp.float32
    )
    acc[:, rows_in:] += lax.dot_general(
        right, basis_out[...], ROWS, preferred_element_type=jnp.float32
    )

    @pl.when(step == pl.num_programs(0) - 1)
    def _():
        out[...] = acc[...]


def rotate(part, own_at, sib_at, own, sib, basis_in, basis_out):
    chips, ranks, wide = own.shape
    wide_in = basis_in.shape[1] // 2 // chips
    wide_out = basis_out.shape[1] // 2 // chips
    rows_in, rows_out = basis_in.shape[0], basis_out.shape[0]
    if wide_in % 128 or wide_out % 128 or rows_in % 128 or rows_out % 128:
        both = jnp.concatenate([jnp.take(own, own_at, 0), jnp.take(sib, sib_at, 0)], axis=1)
        both = both.transpose(1, 0, 2)
        left = both[:, :, :wide_in].reshape(2 * ranks, -1)
        right = both[:, :, wide_in:].reshape(2 * ranks, -1)
        half_in = lax.dynamic_slice_in_dim(basis_in, part * left.shape[1], left.shape[1], 1)
        half_out = lax.dynamic_slice_in_dim(basis_out, part * right.shape[1], right.shape[1], 1)
        return jnp.concatenate(
            [
                lax.dot_general(left, half_in, ROWS, preferred_element_type=jnp.float32),
                lax.dot_general(right, half_out, ROWS, preferred_element_type=jnp.float32),
            ],
            axis=1,
        )
    return pl.pallas_call(
        rotate_kernel,
        grid_spec=pltpu.PrefetchScalarGridSpec(
            num_scalar_prefetch=3,
            grid=(chips,),
            in_specs=[
                pl.BlockSpec((1, ranks, wide), lambda g, part, a, b: (a[g], 0, 0)),
                pl.BlockSpec((1, ranks, wide), lambda g, part, a, b: (b[g], 0, 0)),
                pl.BlockSpec((rows_in, wide_in), lambda g, part, a, b: (0, part[0] * chips + g)),
                pl.BlockSpec((rows_out, wide_out), lambda g, part, a, b: (0, part[0] * chips + g)),
            ],
            out_specs=pl.BlockSpec((2 * ranks, rows_in + rows_out), lambda g, part, a, b: (0, 0)),
            scratch_shapes=[pltpu.VMEM((2 * ranks, rows_in + rows_out), jnp.float32)],
        ),
        out_shape=jax.ShapeDtypeStruct((2 * ranks, rows_in + rows_out), jnp.float32),
        compiler_params=pltpu.CompilerParams(vmem_limit_bytes=32 * 1024 * 1024),
        name="rotate",
    )(part[None], own_at, sib_at, own, sib, basis_in, basis_out)


def project_kernel(part, own_at, sib_at, own, sib, acts, grads, other, mine_out, other_out, acc):
    step = pl.program_id(0)
    wide_in = acts.shape[1]

    @pl.when(step == 0)
    def _():
        acc[...] = jnp.zeros_like(acc)

    left = jnp.concatenate([own[0, :, :wide_in], sib[0, :, :wide_in]], axis=0)
    right = jnp.concatenate([own[0, :, wide_in:], sib[0, :, wide_in:]], axis=0)
    pairs = (
        (acts[...], left),
        (grads[...], right),
        (other[:, :wide_in], left),
        (other[:, wide_in:], right),
    )
    for num, (tokens, factors) in enumerate(pairs):
        acc[num] += lax.dot_general(tokens, factors, ROWS, preferred_element_type=jnp.float32)

    @pl.when(step == pl.num_programs(0) - 1)
    def _():
        mine_out[...] = acc[:2]
        other_out[...] = acc[2:]


def project(part, own_at, sib_at, own, sib, acts, grads, other):
    chips, ranks, wide = own.shape
    tokens = acts.shape[0]
    wide_in, wide_out = acts.shape[1] // 2 // chips, grads.shape[1] // 2 // chips
    if wide_in % 128 or wide_out % 128:
        both = jnp.concatenate([jnp.take(own, own_at, 0), jnp.take(sib, sib_at, 0)], axis=1)

        def dots(left_tokens, right_tokens):
            return jnp.stack(
                [
                    jnp.einsum("tgf,gcf->tc", left_tokens, both[:, :, :wide_in], preferred_element_type=jnp.float32),
                    jnp.einsum("tgf,gcf->tc", right_tokens, both[:, :, wide_in:], preferred_element_type=jnp.float32),
                ]
            )

        left_own = jnp.take(acts.reshape(tokens, chips, 2, wide_in), part, axis=2)
        right_own = jnp.take(grads.reshape(tokens, chips, 2, wide_out), part, axis=2)
        theirs = other.reshape(tokens, chips, wide)
        return dots(left_own, right_own), dots(theirs[:, :, :wide_in], theirs[:, :, wide_in:])
    shape = jax.ShapeDtypeStruct((2, tokens, 2 * ranks), jnp.float32)
    whole = pl.BlockSpec((2, tokens, 2 * ranks), lambda g, part, a, b: (0, 0, 0))
    return pl.pallas_call(
        project_kernel,
        grid_spec=pltpu.PrefetchScalarGridSpec(
            num_scalar_prefetch=3,
            grid=(chips,),
            in_specs=[
                pl.BlockSpec((1, ranks, wide), lambda g, part, a, b: (a[g], 0, 0)),
                pl.BlockSpec((1, ranks, wide), lambda g, part, a, b: (b[g], 0, 0)),
                pl.BlockSpec((tokens, wide_in), lambda g, part, a, b: (0, 2 * g + part[0])),
                pl.BlockSpec((tokens, wide_out), lambda g, part, a, b: (0, 2 * g + part[0])),
                pl.BlockSpec((tokens, wide), lambda g, part, a, b: (0, g)),
            ],
            out_specs=[whole, whole],
            scratch_shapes=[pltpu.VMEM((4, tokens, 2 * ranks), jnp.float32)],
        ),
        out_shape=[shape, shape],
        compiler_params=pltpu.CompilerParams(vmem_limit_bytes=32 * 1024 * 1024),
        name="project",
    )(part[None], own_at, sib_at, own, sib, acts, grads, other)


def orders_of(bits):
    far = list(range(bits - 1, 0, -1))
    if len(far) < 3:
        return far, far[::-1]
    return far, [far[-1]] + far[:-1]


def place_of(order, chips):
    place = [0] * chips
    for spot in range(chips):
        mask = 0
        for level, bit in enumerate(order):
            if spot >> level & 1:
                mask |= 1 << (bit - 1)
        place[mask] = spot
    return place


def xor_gather(piece, orders, count):
    held = piece[None]
    for level in range(len(orders[0])):
        pairs = [(i, i ^ (1 << orders[i & 1][level])) for i in range(count)]
        held = jnp.concatenate([held, lax.ppermute(held, "blk", pairs)], axis=0)
    return held


def swap_cores(value, count):
    return lax.ppermute(value, "blk", [(i, i ^ 1) for i in range(count)])


def shards(
    activations,
    output_grads,
    basis_in,
    basis_out,
    query_left,
    query_right,
    owners,
    lengths,
    slot_plan,
):
    count = lax.axis_size("blk")
    chips = count // 2
    bits = count.bit_length() - 1
    me = lax.axis_index("blk")
    part = lax.axis_index("parts")
    core, chip = me % 2, me // 2
    seqs_here, max_length, width_in = activations.shape
    width_out = output_grads.shape[2]
    num_queries = owners.shape[0]
    rank_count = query_left.shape[1]
    half_rank = rank_count // 2
    tokens = seqs_here * max_length
    acts = activations.reshape(tokens, width_in)
    grads = output_grads.reshape(tokens, width_out)
    everyone = ("parts", "blk")

    orders = orders_of(bits)
    table = jnp.asarray([place_of(order, chips) for order in orders], jnp.int32)
    mask = jnp.arange(chips, dtype=jnp.int32) ^ chip
    own_at = jnp.take(table[core], mask)
    sib_at = jnp.take(table[1 - core], mask)

    away_in = jnp.take(acts.reshape(tokens, chips, 2, -1), 1 - part, axis=2)
    away_out = jnp.take(grads.reshape(tokens, chips, 2, -1), 1 - part, axis=2)
    away = jnp.concatenate([away_in, away_out], axis=2).reshape(tokens, -1)
    across = [(p * count + i, (1 - p) * count + i) for p in range(2) for i in range(count)]
    other = lax.ppermute(away, everyone, across)

    def half(factor):
        wide = factor.shape[2] // 2
        kept = lax.dynamic_slice_in_dim(factor[0], part * wide, wide, 1)
        return kept.reshape(2, half_rank, chips, wide // chips)

    packed = jnp.concatenate([half(query_left), half(query_right)], axis=3)
    packed = packed.transpose(2, 0, 1, 3).reshape(count, half_rank, -1)
    slots = lax.all_to_all(packed, "blk", 0, 0, tiled=True)
    chosen = jnp.take(slots, owners, axis=0).reshape(num_queries * half_rank, -1)
    own = xor_gather(chosen, orders, count)
    sib = swap_cores(own, count)

    partial = rotate(part, own_at, sib_at, own, sib, basis_in, basis_out)
    to_sum = [(p * count + i, (1 - p) * count + i) for p in range(2) for i in range(count) if i % 2 != p]
    arrived = lax.ppermute(partial.astype(jnp.bfloat16), everyone, to_sum)
    summed = (partial + arrived.astype(jnp.float32)).astype(jnp.bfloat16)
    ranks = num_queries * half_rank
    to_core = [(p * count + i, p * count + (i ^ 1)) for p in range(2) for i in range(count) if i % 2 == p]
    given = lax.ppermute(summed[ranks:], everyone, to_core)
    piece = jnp.where(core == part, summed[:ranks], given)
    own_rotated = xor_gather(piece, orders, count)
    sib_rotated = swap_cores(own_rotated, count)

    mine, theirs = project(part, own_at, sib_at, own_rotated, sib_rotated, acts, grads, other)
    mine = mine + lax.ppermute(theirs, everyone, across)

    seqs = me * seqs_here + jnp.arange(seqs_here, dtype=jnp.int32)
    live = jnp.arange(max_length, dtype=jnp.int32)[None, :] < lengths[slot_plan[seqs]][:, None]
    products = (mine[0] * mine[1]).reshape(seqs_here, max_length, -1)
    sums = jnp.sum(jnp.where(live[:, :, None], products, 0.0), axis=1)
    held = (jnp.sum(sums.reshape(seqs_here, 2, num_queries, half_rank), axis=(1, 3)) / rank_count)[None]
    for bit in range(bits):
        pairs = [(i, i ^ (1 << bit)) for i in range(count)]
        held = jnp.concatenate([held, lax.ppermute(held, "blk", pairs)], axis=0)
    from_device = jnp.arange(count, dtype=jnp.int32) ^ me
    planned = slot_plan.reshape(count, seqs_here)[from_device]
    chooser = planned[None, :, :] == seqs[:, None, None]
    return jnp.sum(jnp.where(chooser[..., None], held[None], 0.0), axis=(1, 2))


def solution(mesh):
    placed = (
        P(("parts", "blk"), None, None),
        P(("parts", "blk"), None, None),
        P("blk", None),
        P("blk", None),
        P("blk", None, None),
        P("blk", None, None),
        P(),
        P("parts"),
        P("parts"),
    )
    return jax.shard_map(
        shards, mesh=mesh, in_specs=placed, out_specs=P(("parts", "blk"), None), check_vma=False
    )
```

```python
import jax
import jax.numpy as jnp
from jax import lax
from jax.experimental import pallas as pl
from jax.experimental.pallas import tpu as pltpu
from jax.sharding import PartitionSpec as P

ROWS = (((1,), (1,)), ((), ()))
EVERYONE = ("parts", "blk")
NEAR = 4
CHAINS = 2
MIB = 1024 * 1024


def dot_rows(left, right):
    return lax.dot_general(left, right, ROWS, preferred_element_type=jnp.float32)


def swapped(spot, bits):
    top, second = 1 << (bits - 1), 1 << (bits - 2)
    rest = spot & (second - 1)
    return rest | (second if spot & top else 0) | (top if spot & second else 0)


def masks_of(bits):
    steps = list(range(bits - 1, 1, -1))
    walks = (steps + [1, 0], steps + [0, 1])
    return walks, [
        [sum(1 << bit for level, bit in enumerate(walk) if spot >> level & 1) for spot in range(1 << bits)]
        for walk in walks
    ]


def pick(low, high, spot):
    half = low.shape[0]
    return low[spot] if spot < half else high[spot - half]


def rotate(part, chunks, chain, factors, bases, rows, total, last):
    own_low, own_high, sib_low, sib_high = factors
    ranks, wide = own_low.shape[1:]
    wide_in = bases[0].shape[1] // (2 * CHAINS * NEAR)
    wide_out = wide - wide_in
    (in_from, in_to), (out_from, out_to) = rows
    count_in, count_out = in_to - in_from, out_to - out_from
    height = count_in + count_out
    if height % 128 or wide_in % 128 or wide_out % 128:
        own = jnp.concatenate([own_low, own_high], axis=0)
        sib = jnp.concatenate([sib_low, sib_high], axis=0)[jnp.array([swapped(s, 2) for s in range(NEAR)])]
        both = jnp.concatenate([own, sib], axis=1)
        both = jnp.take(both, jnp.argsort(chunks), axis=0).transpose(1, 0, 2)
        result = []
        for basis, begin, end, lanes in (
            (bases[0], in_from, in_to, both[:, :, :wide_in]),
            (bases[1], out_from, out_to, both[:, :, wide_in:]),
        ):
            flat = lanes.reshape(2 * ranks, -1)
            kept = lax.dynamic_slice_in_dim(basis[begin:end], (part * CHAINS + chain) * flat.shape[1], flat.shape[1], 1)
            result.append(dot_rows(flat, kept))
        result = jnp.concatenate(result, axis=1)
        if total is not None:
            result = result + total
        return (result, result.astype(jnp.bfloat16)) if last else result

    def kernel(where, low, high, slow, shigh, basis_in, basis_out, *rest):
        if total is not None:
            start, rest = rest[0], rest[1:]
        outs, (buf_in, buf_out, acc, sems) = rest[:-4], rest[-4:]
        base = where[0] * CHAINS + chain
        copies = []
        for spot in range(NEAR):
            column = base * NEAR + where[1 + spot]
            pair = []
            if count_in:
                lanes = pl.ds(pl.multiple_of(column * wide_in, 128), wide_in)
                pair.append(
                    pltpu.make_async_copy(
                        basis_in.at[pl.ds(in_from, count_in), lanes], buf_in.at[spot], sems.at[0, spot]
                    )
                )
            if count_out:
                lanes = pl.ds(pl.multiple_of(column * wide_out, 128), wide_out)
                pair.append(
                    pltpu.make_async_copy(
                        basis_out.at[pl.ds(out_from, count_out), lanes], buf_out.at[spot], sems.at[1, spot]
                    )
                )
            for copy in pair:
                copy.start()
            copies.append(pair)
        for spot in range(NEAR):
            factor = jnp.concatenate([pick(low, high, spot), pick(slow, shigh, swapped(spot, 2))], axis=0)
            for copy in copies[spot]:
                copy.wait()
            if count_in:
                value = dot_rows(buf_in[spot], factor[:, :wide_in])
                acc[:count_in] = value if spot == 0 else acc[:count_in] + value
            if count_out:
                value = dot_rows(buf_out[spot], factor[:, wide_in:])
                acc[count_in:] = value if spot == 0 else acc[count_in:] + value
        value = acc[...].T
        if total is not None:
            value = value + start[...]
        outs[0][...] = value
        if last:
            outs[1][...] = value.astype(jnp.bfloat16)

    vmem = pl.BlockSpec(memory_space=pltpu.VMEM)
    hbm = pl.BlockSpec(memory_space=pl.ANY)
    shapes = [jax.ShapeDtypeStruct((2 * ranks, height), jnp.float32)]
    if last:
        shapes.append(jax.ShapeDtypeStruct((2 * ranks, height), jnp.bfloat16))
    given = [] if total is None else [total]
    results = pl.pallas_call(
        kernel,
        in_specs=[pl.BlockSpec(memory_space=pltpu.SMEM)] + [vmem] * 4 + [hbm] * 2 + [vmem] * len(given),
        out_specs=[vmem] * len(shapes),
        out_shape=shapes,
        scratch_shapes=[
            pltpu.VMEM((NEAR, max(count_in, 16), wide_in), jnp.bfloat16),
            pltpu.VMEM((NEAR, max(count_out, 16), wide_out), jnp.bfloat16),
            pltpu.VMEM((height, 2 * ranks), jnp.float32),
            pltpu.SemaphoreType.DMA((2, NEAR)),
        ],
        compiler_params=pltpu.CompilerParams(vmem_limit_bytes=20 * MIB),
        cost_estimate=pl.CostEstimate(
            flops=4 * ranks * NEAR * (count_in * wide_in + count_out * wide_out),
            bytes_accessed=2 * NEAR * (count_in * wide_in + count_out * wide_out),
            transcendentals=0,
        ),
        name="rotate",
    )(jnp.concatenate([part[None], chunks]), *factors, *bases, *given)
    return tuple(results) if last else results[0]


def project(part, chip_at, factors, lanes, acts, grads, other, totals, bits):
    chips = 1 << bits
    own_low, own_high, sib_low, sib_high = factors
    ranks = own_low.shape[1]
    tokens = acts.shape[0]
    wide_in, wide_out = acts.shape[1] // 2 // chips, grads.shape[1] // 2 // chips
    wide = wide_in + wide_out
    begin, end = lanes
    cut = min(max(wide_in - begin, 0), end - begin)
    has_in, has_out = cut > 0, cut < end - begin
    out_from, out_to = max(begin - wide_in, 0), end - wide_in
    names = [num for num, used in enumerate((has_in, has_out)) if used]
    if wide_in % 128 or wide_out % 128:
        order = jnp.array([swapped(s, bits) for s in range(chips)])
        own = jnp.concatenate([own_low, own_high], axis=0)
        sib = jnp.concatenate([sib_low, sib_high], axis=0)[order]
        both = jnp.take(jnp.concatenate([own, sib], axis=1), jnp.argsort(chip_at), axis=0)
        sides = []
        theirs = other.reshape(tokens, chips, wide)
        mine = jnp.concatenate(
            [
                jnp.take(acts.reshape(tokens, chips, 2, wide_in), part, axis=2),
                jnp.take(grads.reshape(tokens, chips, 2, wide_out), part, axis=2),
            ],
            axis=2,
        )
        for held in (mine, theirs):
            for piece in (slice(0, wide_in), slice(wide_in, wide)):
                sides.append(
                    jnp.einsum("tgf,gcf->tc", held[:, :, piece], both[:, :, piece], preferred_element_type=jnp.float32)
                )
        return jnp.stack(sides).reshape(2, 2, tokens, 2 * ranks)

    def kernel(where, low, high, slow, shigh, acts, grads, other, *rest):
        if totals is not None:
            start, rest = rest[0], rest[1:]
        out = rest[0]
        step = pl.program_id(0)

        @pl.when(step == 0)
        def _():
            out[...] = jnp.zeros_like(out) if totals is None else start[...]

        for spot in range(chips):

            @pl.when(step == spot)
            def _():
                factor = jnp.concatenate([pick(low, high, spot), pick(slow, shigh, swapped(spot, bits))], axis=0)
                if has_in:
                    out[0, 0] += dot_rows(acts[...], factor[:, :cut])
                    out[1, 0] += dot_rows(other[:, begin : begin + cut], factor[:, :cut])
                if has_out:
                    out[0, 1] += dot_rows(grads[:, out_from:out_to], factor[:, cut:])
                    out[1, 1] += dot_rows(other[:, wide_in + out_from : wide_in + out_to], factor[:, cut:])

    shape = (2, 2, tokens, 2 * ranks)
    full = lambda array: pl.BlockSpec(array.shape, lambda s, w: (0,) * array.ndim)
    given = [] if totals is None else [totals]
    return pl.pallas_call(
        kernel,
        grid_spec=pltpu.PrefetchScalarGridSpec(
            num_scalar_prefetch=1,
            grid=(chips,),
            in_specs=[full(factor) for factor in factors]
            + [
                pl.BlockSpec((tokens, wide_in), lambda s, w: (0, 2 * w[1 + s] + w[0])),
                pl.BlockSpec((tokens, wide_out), lambda s, w: (0, 2 * w[1 + s] + w[0])),
                pl.BlockSpec((tokens, wide), lambda s, w: (0, w[1 + s])),
            ]
            + [full(total) for total in given],
            out_specs=pl.BlockSpec(shape, lambda s, w: (0, 0, 0, 0)),
        ),
        out_shape=jax.ShapeDtypeStruct(shape, jnp.float32),
        compiler_params=pltpu.CompilerParams(vmem_limit_bytes=20 * MIB),
        cost_estimate=pl.CostEstimate(
            flops=8 * tokens * ranks * chips * (end - begin),
            bytes_accessed=4 * tokens * chips * (end - begin),
            transcendentals=0,
        ),
        name="project",
    )(jnp.concatenate([part[None], chip_at]), *factors, acts, grads, other, *given)


def features_away(part, acts, grads, chips):
    tokens = acts.shape[0]
    wide_in, wide_out = acts.shape[1] // 2 // chips, grads.shape[1] // 2 // chips
    if wide_in % 128 or wide_out % 128:
        away_in = jnp.take(acts.reshape(tokens, chips, 2, wide_in), 1 - part, axis=2)
        away_out = jnp.take(grads.reshape(tokens, chips, 2, wide_out), 1 - part, axis=2)
        return jnp.concatenate([away_in, away_out], axis=2).reshape(tokens, -1)

    def kernel(where, acts, grads, out):
        out[:, :wide_in] = acts[...]
        out[:, wide_in:] = grads[...]

    wide = wide_in + wide_out
    return pl.pallas_call(
        kernel,
        grid_spec=pltpu.PrefetchScalarGridSpec(
            num_scalar_prefetch=1,
            grid=(chips,),
            in_specs=[
                pl.BlockSpec((tokens, wide_in), lambda g, w: (0, 2 * g + 1 - w[0])),
                pl.BlockSpec((tokens, wide_out), lambda g, w: (0, 2 * g + 1 - w[0])),
            ],
            out_specs=pl.BlockSpec((tokens, wide), lambda g, w: (0, g)),
        ),
        out_shape=jax.ShapeDtypeStruct((tokens, chips * wide), acts.dtype),
        cost_estimate=pl.CostEstimate(flops=0, bytes_accessed=4 * tokens * chips * wide, transcendentals=0),
        name="features_away",
    )(part[None], acts, grads)


def shards(
    activations,
    output_grads,
    basis_in,
    basis_out,
    query_left,
    query_right,
    owners,
    lengths,
    slot_plan,
):
    count = lax.axis_size("blk")
    chips = count // 2
    bits = chips.bit_length() - 1
    me = lax.axis_index("blk")
    part = lax.axis_index("parts")
    core, chip = me % 2, me // 2
    seqs_here, max_length, width_in = activations.shape
    num_queries = owners.shape[0]
    rank_count = query_left.shape[1]
    half_rank = rank_count // 2
    ranks = num_queries * half_rank
    tokens = seqs_here * max_length
    acts = activations.reshape(tokens, width_in)
    grads = output_grads.reshape(tokens, -1)
    across = [(p * count + i, (1 - p) * count + i) for p in range(2) for i in range(count)]

    def to_chip(value, mask):
        return lax.ppermute(value, "blk", [(i, i ^ (2 * mask)) for i in range(count)])

    def along(value, first, second):
        return lax.ppermute(value, "blk", [(i, i ^ (2 << (second if i % 2 else first))) for i in range(count)])

    def to_core(value):
        return lax.ppermute(value, "blk", [(i, i ^ 1) for i in range(count)])

    walks, masks = masks_of(bits)
    chip_at = jnp.where(core == 0, jnp.array(masks[0], jnp.int32), jnp.array(masks[1], jnp.int32)) ^ chip
    _, near_masks = masks_of(2)
    near_at = jnp.where(core == 0, jnp.array(near_masks[0], jnp.int32), jnp.array(near_masks[1], jnp.int32)) ^ (
        chip % NEAR
    )

    def half(factor):
        wide = factor.shape[2] // 2
        kept = lax.dynamic_slice_in_dim(factor[0], part * wide, wide, 1)
        return kept.reshape(2, half_rank, CHAINS, NEAR, wide // (CHAINS * NEAR))

    packed = jnp.concatenate([half(query_left), half(query_right)], axis=4).transpose(0, 3, 2, 1, 4)
    mine = jnp.take(packed, core, axis=0)
    slot_pair = jnp.stack([mine, to_core(jnp.take(packed, 1 - core, axis=0))], axis=1)
    messages = [jnp.take(slot_pair, (chip % NEAR) ^ mask, axis=0) for mask in range(NEAR)]
    found = [messages[0]] + [to_chip(messages[mask], mask) for mask in range(1, NEAR)]

    acts_late, grads_late, *_ = lax.optimization_barrier((acts, grads, *messages))
    other = lax.ppermute(features_away(part, acts_late, grads_late, chips), EVERYONE, across)

    source = (owners // 2) ^ chip
    spot = jnp.minimum(source, NEAR - 1) * 2 + ((owners % 2) ^ core)
    known = (source < NEAR)[:, None, None]
    slots = jnp.concatenate(found, axis=0)
    gathered = []
    for chain in range(CHAINS):
        dense = jnp.where(known, jnp.take(slots[:, chain], spot, axis=0), 0).reshape(1, ranks, -1)
        for bit in range(bits - 1, 1, -1):
            dense = dense + to_chip(dense, 1 << bit)
        low = jnp.concatenate([dense, along(dense, 1, 0)], axis=0)
        high = along(low, 0, 1)
        gathered.append((low, high, to_core(low), to_core(high)))

    rows_in, rows_out = basis_in.shape[0], basis_out.shape[0]
    wide = rows_in + rows_out
    first = (wide // 128 + 1) // 2 * 128
    splits = [(0, wide)] if rows_in % 128 or rows_out % 128 or first <= rows_in else [(0, first), (first, wide)]
    bases = (basis_in, basis_out)
    everything = ((0, rows_in), (0, rows_out))
    total = None
    for chain in range(CHAINS - 1):
        total = rotate(part, near_at, chain, gathered[chain], bases, everything, total, False)
    to_sum = [(p * count + i, (1 - p) * count + i) for p in range(2) for i in range(count) if i % 2 != p]
    to_half = [(p * count + i, p * count + (i ^ 1)) for p in range(2) for i in range(count) if i % 2 == p]
    projected = None
    for begin, end in splits:
        rows = (
            (min(begin, rows_in), min(end, rows_in)),
            (max(begin - rows_in, 0), max(end - rows_in, 0)),
        )
        so_far = None if total is None else total[:, begin:end]
        partial, sent = rotate(part, near_at, CHAINS - 1, gathered[-1], bases, rows, so_far, True)
        arrived = lax.ppermute(sent, EVERYONE, to_sum)
        summed = (partial + arrived.astype(jnp.float32)).astype(jnp.bfloat16)
        given = lax.ppermute(summed[ranks:], EVERYONE, to_half)
        low = jnp.where(core == part, summed[:ranks], given)[None]
        for level in range(bits - 1):
            low = jnp.concatenate([low, along(low, walks[0][level], walks[1][level])], axis=0)
        high = along(low, walks[0][-1], walks[1][-1])
        factors = (low, high, to_core(low), to_core(high))
        projected = project(part, chip_at, factors, (begin, end), acts, grads, other, projected, bits)

    mine = projected[0] + lax.ppermute(projected[1], EVERYONE, across)
    seqs = me * seqs_here + jnp.arange(seqs_here, dtype=jnp.int32)
    live = jnp.arange(max_length, dtype=jnp.int32)[None, :] < lengths[slot_plan[seqs]][:, None]
    products = (mine[0] * mine[1]).reshape(seqs_here, max_length, -1)
    sums = jnp.sum(jnp.where(live[:, :, None], products, 0.0), axis=1)
    held = (jnp.sum(sums.reshape(seqs_here, 2, num_queries, half_rank), axis=(1, 3)) / rank_count)[None]
    for bit in range(bits + 1):
        pairs = [(i, i ^ (1 << bit)) for i in range(count)]
        held = jnp.concatenate([held, lax.ppermute(held, "blk", pairs)], axis=0)
    from_device = jnp.arange(count, dtype=jnp.int32) ^ me
    planned = slot_plan.reshape(count, seqs_here)[from_device]
    chooser = planned[None, :, :] == seqs[:, None, None]
    return jnp.sum(jnp.where(chooser[..., None], held[None], 0.0), axis=(1, 2))


def solution(mesh):
    placed = (
        P(("parts", "blk"), None, None),
        P(("parts", "blk"), None, None),
        P("blk", None),
        P("blk", None),
        P("blk", None, None),
        P("blk", None, None),
        P(),
        P("parts"),
        P("parts"),
    )
    return jax.shard_map(
        shards, mesh=mesh, in_specs=placed, out_specs=P(("parts", "blk"), None), check_vma=False
    )
```

```python
import jax
import jax.numpy as jnp
from jax import lax
from jax.experimental import pallas as pl
from jax.experimental.pallas import tpu as pltpu
from jax.sharding import PartitionSpec as P

ROWS = (((1,), (1,)), ((), ()))
EVERYONE = ("parts", "blk")
NEAR = 4
CHAINS = 2
SHARES = (2, 3, 3)
MIB = 1024 * 1024


def dot_rows(left, right):
    return lax.dot_general(left, right, ROWS, preferred_element_type=jnp.float32)


NEAR_MASKS = ((0, 1, 2, 3), (0, 2, 1, 3))
SIBLING = (0, 2, 1, 3)


def after(values, other):
    return list(lax.optimization_barrier((*values, other)))[:-1]


VMEM = pl.BlockSpec(memory_space=pltpu.VMEM)
SMEM = pl.BlockSpec(memory_space=pltpu.SMEM)
HBM = pl.BlockSpec(memory_space=pltpu.HBM)


def in_hbm(value):
    return pltpu.with_memory_space_constraint(value, pltpu.HBM)


def in_vmem(value):
    return pltpu.with_memory_space_constraint(value, pltpu.VMEM)


def lanes_at(number, width):
    return pl.ds(pl.multiple_of(number * width, 128), width)


def copy_all(copies):
    for copy in copies:
        copy.start()
    for copy in copies:
        copy.wait()


def estimate(flops, moved):
    return pl.CostEstimate(flops=flops, bytes_accessed=moved, transcendentals=0)


def rank_halves(part, core, left, right):
    half_rank = left.shape[1] // 2
    widths = [factor.shape[2] // (2 * CHAINS * NEAR) for factor in (left, right)]
    wide = sum(widths)

    def kernel(where, left, right, away, kept, sems):
        copies = []
        for side, out in enumerate((away, kept)):
            rows = pl.ds(pl.multiple_of((where[1] if side else 1 - where[1]) * half_rank, half_rank), half_rank)
            for chunk in range(NEAR):
                for chain in range(CHAINS):
                    number = (where[0] * CHAINS + chain) * NEAR + chunk
                    target = out.at[chunk, chain]
                    copies.append(
                        pltpu.make_async_copy(
                            left.at[0, rows, lanes_at(number, widths[0])],
                            target.at[:, pl.ds(0, widths[0])],
                            sems.at[len(copies)],
                        )
                    )
                    copies.append(
                        pltpu.make_async_copy(
                            right.at[0, rows, lanes_at(number, widths[1])],
                            target.at[:, pl.ds(widths[0], widths[1])],
                            sems.at[len(copies)],
                        )
                    )
        copy_all(copies)

    shape = (NEAR, CHAINS, half_rank, wide)
    return pl.pallas_call(
        kernel,
        in_specs=[SMEM, HBM, HBM],
        out_specs=[VMEM] * 2,
        out_shape=[pltpu.VMEM(shape, left.dtype)] * 2,
        scratch_shapes=[pltpu.SemaphoreType.DMA((4 * NEAR * CHAINS,))],
        compiler_params=pltpu.CompilerParams(vmem_limit_bytes=4 * MIB),
        cost_estimate=estimate(0, 8 * NEAR * CHAINS * half_rank * wide),
        name="rank_halves",
    )(jnp.stack([part, core]), in_hbm(left), in_hbm(right))


def messages_of(spot, kept, received):
    def kernel(where, kept, received, *outs):
        for chain in range(CHAINS):
            for mask in range(NEAR):
                chunk = where[0] ^ mask
                outs[chain * NEAR + mask][0] = kept[chunk, chain]
                outs[chain * NEAR + mask][1] = received[chunk, chain]

    shape = jax.ShapeDtypeStruct((2,) + kept.shape[2:], kept.dtype)
    outs = pl.pallas_call(
        kernel,
        in_specs=[SMEM, VMEM, VMEM],
        out_specs=[VMEM] * (NEAR * CHAINS),
        out_shape=[shape] * (NEAR * CHAINS),
        compiler_params=pltpu.CompilerParams(vmem_limit_bytes=4 * MIB),
        cost_estimate=estimate(0, 4 * 2 * kept.size),
        name="messages",
    )(spot[None], kept, received)
    return [outs[chain * NEAR : (chain + 1) * NEAR] for chain in range(CHAINS)]


def chunk_copies(number, bases, targets, widths, rows, sems):
    copies = []
    for num, (basis, target, width, (begin, end)) in enumerate(zip(bases, targets, widths, rows)):
        if end > begin:
            source = basis.at[pl.ds(begin, end - begin), lanes_at(number, width)]
            copies.append(pltpu.make_async_copy(source, target, sems.at[num]))
    return copies


def stage_bases(part, bases):
    widths = [basis.shape[1] // (2 * CHAINS) for basis in bases]
    rows = [(0, basis.shape[0]) for basis in bases]

    def kernel(where, first, second, first_out, second_out, sems):
        number = where[0] * CHAINS + CHAINS - 1
        copy_all(chunk_copies(number, (first, second), (first_out, second_out), widths, rows, sems))

    shapes = [(basis.shape[0], width) for basis, width in zip(bases, widths)]
    return pl.pallas_call(
        kernel,
        in_specs=[SMEM, HBM, HBM],
        out_specs=[VMEM] * 2,
        out_shape=[pltpu.VMEM(shape, bases[0].dtype) for shape in shapes],
        scratch_shapes=[pltpu.SemaphoreType.DMA((2,))],
        compiler_params=pltpu.CompilerParams(vmem_limit_bytes=4 * MIB),
        cost_estimate=estimate(0, 2 * sum(shape[0] * shape[1] for shape in shapes)),
        name="stage_bases",
    )(part[None], *map(in_hbm, bases))


def choose(spot, found):
    queries = spot.shape[0]
    ranks, wide = found[0].shape[1:]

    def kernel(where, *rest):
        out = rest[-1]
        for query in range(queries):
            place = pl.ds(query * ranks, ranks)
            for mask in range(NEAR):

                @pl.when(where[query] // 2 == mask)
                def _():
                    out[0, place] = rest[mask][where[query] % 2]

            @pl.when(where[query] >= 2 * NEAR)
            def _():
                out[0, place] = jnp.zeros((ranks, wide), out.dtype)

    return pl.pallas_call(
        kernel,
        in_specs=[SMEM] + [VMEM] * NEAR,
        out_specs=VMEM,
        out_shape=jax.ShapeDtypeStruct((1, queries * ranks, wide), found[0].dtype),
        compiler_params=pltpu.CompilerParams(vmem_limit_bytes=4 * MIB),
        cost_estimate=estimate(0, 4 * queries * ranks * wide),
        name="choose",
    )(spot, *found)


def features_of(part, chip_at, acts, grads, pieces):
    tokens, chips = acts.shape[0], chip_at.shape[0]
    wide_in, wide_out = acts.shape[1] // 2 // chips, grads.shape[1] // 2 // chips
    wide = wide_in + wide_out
    if wide_in % 128 or wide_out % 128:
        some_in = jnp.take(jnp.take(acts.reshape(tokens, chips, 2, wide_in), part, axis=2), chip_at, axis=1)
        some_out = jnp.take(jnp.take(grads.reshape(tokens, chips, 2, wide_out), part, axis=2), chip_at, axis=1)
        some = jnp.concatenate([some_in, some_out], axis=2)
        return [some[:, begin:end].reshape(tokens, -1) for begin, end in pieces]
    total = sum(end - begin for begin, end in pieces)

    def kernel(where, acts, grads, *rest):
        outs, sems = rest[:-1], rest[-1]
        copies = []
        for out, (first, last) in zip(outs, pieces):
            for spot in range(first, last):
                number = 2 * where[1 + spot] + where[0]
                for source, width, begin in ((acts, wide_in, 0), (grads, wide_out, wide_in)):
                    copies.append(
                        pltpu.make_async_copy(
                            source.at[:, lanes_at(number, width)],
                            out.at[:, pl.ds((spot - first) * wide + begin, width)],
                            sems.at[len(copies)],
                        )
                    )
        copy_all(copies)

    return pl.pallas_call(
        kernel,
        in_specs=[SMEM, HBM, HBM],
        out_specs=[VMEM] * len(pieces),
        out_shape=[pltpu.VMEM((tokens, (end - begin) * wide), acts.dtype) for begin, end in pieces],
        scratch_shapes=[pltpu.SemaphoreType.DMA((2 * total,))],
        compiler_params=pltpu.CompilerParams(vmem_limit_bytes=4 * MIB),
        cost_estimate=estimate(0, 4 * tokens * total * wide),
        name="features",
    )(jnp.concatenate([part[None], chip_at]), in_hbm(acts), in_hbm(grads))


def rotate(part, chunks, chain, factors, bases, rows, total):
    last = chain == CHAINS - 1
    ranks, wide = factors[0].shape
    wide_in = bases[0].shape[1] // NEAR if last else bases[0].shape[1] // (2 * CHAINS * NEAR)
    widths = (wide_in, wide - wide_in)
    counts = [end - begin for begin, end in rows]
    height = sum(counts)
    spans = [(0, counts[0], 0, wide_in), (counts[0], height, wide_in, wide)]

    def kernel(where, *rest):
        own, sib, (basis_in, basis_out), rest = rest[:NEAR], rest[NEAR : 2 * NEAR], rest[2 * NEAR :][:2], rest[2 * NEAR + 2 :]
        if total is not None:
            start, rest = rest[0], rest[1:]
        if last:
            outs, acc = rest[:-1], rest[-1]
        else:
            outs, (buf_in, buf_out, acc, sems) = rest[:-4], rest[-4:]
            copies = []
            for spot in range(NEAR):
                number = (where[0] * CHAINS + chain) * NEAR + where[1 + spot]
                targets = (buf_in.at[spot], buf_out.at[spot])
                copies.append(
                    chunk_copies(number, (basis_in, basis_out), targets, widths, rows, sems.at[spot])
                )
                for copy in copies[spot]:
                    copy.start()
        for spot in range(NEAR):
            factor = jnp.concatenate([own[spot][...], sib[SIBLING[spot]][...]], axis=0)
            if not last:
                for copy in copies[spot]:
                    copy.wait()
            for num, (from_row, to_row, from_lane, to_lane) in enumerate(spans):
                if to_row == from_row:
                    continue
                if last:
                    basis = (basis_in, basis_out)[num]
                    block = basis[rows[num][0] : rows[num][1], lanes_at(where[1 + spot], widths[num])]
                else:
                    block = (buf_in, buf_out)[num][spot]
                value = dot_rows(block, factor[:, from_lane:to_lane])
                acc[from_row:to_row] = value if spot == 0 else acc[from_row:to_row] + value
        value = acc[...]
        if total is not None:
            value = value + start[...]
        if last:
            value = value.T
            outs[1][...] = value.astype(jnp.bfloat16)
        outs[0][...] = value

    if last:
        shapes = [jax.ShapeDtypeStruct((2 * ranks, height), kind) for kind in (jnp.float32, jnp.bfloat16)]
        scratch = []
        place, operands = VMEM, map(in_vmem, bases)
    else:
        shapes = [jax.ShapeDtypeStruct((height, 2 * ranks), jnp.float32)]
        scratch = [pltpu.VMEM((NEAR, count, width), jnp.bfloat16) for count, width in zip(counts, widths)]
        place, operands = HBM, map(in_hbm, bases)
    scratch.append(pltpu.VMEM((height, 2 * ranks), jnp.float32))
    if not last:
        scratch.append(pltpu.SemaphoreType.DMA((NEAR, 2)))
    given = [] if total is None else [total]
    moved = sum(count * width for count, width in zip(counts, widths))
    results = pl.pallas_call(
        kernel,
        in_specs=[SMEM] + [VMEM] * (2 * NEAR) + [place] * 2 + [VMEM] * len(given),
        out_specs=[VMEM] * len(shapes),
        out_shape=shapes,
        scratch_shapes=scratch,
        compiler_params=pltpu.CompilerParams(vmem_limit_bytes=(4 if last else 12) * MIB),
        cost_estimate=estimate(4 * ranks * NEAR * moved, 2 * NEAR * moved),
        name="rotate",
    )(jnp.concatenate([part[None], chunks]), *factors, *operands, *given)
    return tuple(results) if last else results[0]


def project(own, sib, wide_in, tokens_in, pieces, kind):
    chips = len(own)
    ranks, wide = own[0].shape
    tokens = tokens_in[0].shape[0]
    if wide_in % 128 or wide % 128:
        both = jnp.stack([jnp.concatenate(pair, axis=0) for pair in zip(own, sib)])
        held = jnp.concatenate(tokens_in, axis=1).reshape(tokens, chips, wide)
        return [
            jnp.einsum("tgf,gcf->tc", held[:, :, lanes], both[:, :, lanes], preferred_element_type=jnp.float32).astype(
                kind
            )
            for lanes in (slice(0, wide_in), slice(wide_in, wide))
        ]
    staged = len(tokens_in) == 1

    def kernel(*rest):
        factors, rest = rest[: 2 * chips], rest[2 * chips :]
        held, rest = rest[: len(tokens_in)], rest[len(tokens_in) :]
        outs, acc = rest[:2], rest[2]
        if not staged:
            buffer, sems = rest[3:]
            copies = []
            for source, (first, last) in zip(held, pieces):
                for spot in range(first, last):
                    block = source.at[:, pl.ds((spot - first) * wide, wide)]
                    copies.append(pltpu.make_async_copy(block, buffer.at[spot], sems.at[spot]))
                    copies[-1].start()
        for spot in range(chips):
            factor = jnp.concatenate([factors[spot][...], factors[chips + spot][...]], axis=0)
            if not staged:
                copies[spot].wait()
            for num, (begin, end) in enumerate(((0, wide_in), (wide_in, wide))):
                block = held[0][:, spot * wide + begin : spot * wide + end] if staged else buffer[spot, :, begin:end]
                value = dot_rows(block, factor[:, begin:end])
                acc[num] = value if spot == 0 else acc[num] + value
        for num, out in enumerate(outs):
            out[...] = acc[num].astype(kind)

    scratch = [pltpu.VMEM((2, tokens, 2 * ranks), jnp.float32)]
    if not staged:
        scratch += [pltpu.VMEM((chips, tokens, wide), own[0].dtype), pltpu.SemaphoreType.DMA((chips,))]
    return pl.pallas_call(
        kernel,
        in_specs=[VMEM] * (2 * chips) + [VMEM if staged else HBM] * len(tokens_in),
        out_specs=[VMEM] * 2,
        out_shape=[jax.ShapeDtypeStruct((tokens, 2 * ranks), kind)] * 2,
        scratch_shapes=scratch,
        compiler_params=pltpu.CompilerParams(vmem_limit_bytes=(4 if staged else 8) * MIB),
        cost_estimate=estimate(4 * tokens * ranks * chips * wide, 4 * ranks * chips * wide),
        name="project",
    )(*own, *sib, *map(in_vmem if staged else in_hbm, tokens_in))


def shards(
    activations,
    output_grads,
    basis_in,
    basis_out,
    query_left,
    query_right,
    owners,
    lengths,
    slot_plan,
):
    count = lax.axis_size("blk")
    chips = count // 2
    bits = chips.bit_length() - 1
    me = lax.axis_index("blk")
    part = lax.axis_index("parts")
    core, chip = me % 2, me // 2
    seqs_here, max_length, width_in = activations.shape
    num_queries = owners.shape[0]
    rank_count = query_left.shape[1]
    half_rank = rank_count // 2
    ranks = num_queries * half_rank
    tokens = seqs_here * max_length
    acts = activations.reshape(tokens, width_in)
    grads = output_grads.reshape(tokens, -1)
    across = [(p * count + i, (1 - p) * count + i) for p in range(2) for i in range(count)]

    def to_chip(value, mask):
        return lax.ppermute(value, "blk", [(i, i ^ (2 * mask)) for i in range(count)])

    def along(value, first, second):
        return lax.ppermute(value, "blk", [(i, i ^ (2 << (second if i % 2 else first))) for i in range(count)])

    def to_core(value):
        return lax.ppermute(value, "blk", [(i, i ^ 1) for i in range(count)])

    def near_gather(value):
        first = along(value, 0, 1)
        second = along(value, 1, 0)
        return [value, first, second, along(first, 1, 0)]

    near_at = jnp.where(core == 0, jnp.array(NEAR_MASKS[0], jnp.int32), jnp.array(NEAR_MASKS[1], jnp.int32)) ^ (
        chip % NEAR
    )
    sources = [[0]]
    for bit in range(2, bits):
        sources.append([mask | (1 << bit) for group in sources for mask in group])
    orders = [[far | near for group in sources for near in NEAR_MASKS[side] for far in group] for side in range(2)]
    chip_at = jnp.where(core == 0, jnp.array(orders[0], jnp.int32), jnp.array(orders[1], jnp.int32)) ^ chip

    away, kept = rank_halves(part, core, query_left, query_right)
    messages = messages_of(chip % NEAR, kept, to_core(away))
    shares = [chips * sum(SHARES[:num]) // sum(SHARES) for num in range(len(SHARES) + 1)]
    pieces = list(zip(shares[:-1], shares[1:]))

    def give_away(num, other):
        (piece,) = features_of(1 - part, chip_at, *after((acts, grads), other), pieces[num : num + 1])
        return piece

    others = [lax.ppermute(give_away(0, messages[0][0]), EVERYONE, across)]

    source = (owners // 2) ^ chip
    spot = jnp.where(source < NEAR, source * 2 + ((owners % 2) ^ core), 2 * NEAR)
    every = range(CHAINS)
    found = [[to_chip(group[mask], mask) if mask else group[0] for mask in range(NEAR)] for group in messages]
    dense = []
    for chain in every:
        if chain:
            found[chain] = after(found[chain], dense[chain - 1])
        dense.append(choose(spot, found[chain]))
    bases = stage_bases(part, after((basis_in, basis_out), dense[0]))
    for bit in range(bits - 1, 1, -1):
        arrived = [to_chip(dense[chain], 1 << bit) for chain in every]
        for chain in every:
            if chain:
                (arrived[chain],) = after((arrived[chain],), dense[chain - 1])
            dense[chain] = dense[chain] + arrived[chain]
    others.append(lax.ppermute(give_away(1, bases[0]), EVERYONE, across))
    others[0], dense[0], *bases = lax.optimization_barrier((others[0], dense[0], *bases))
    gathered = []
    for chain in every:
        own = near_gather(dense[chain][0])
        if chain:
            own[1:3] = after(own[1:3], gathered[0][0][1])
        if chain == CHAINS - 1:
            own[3], others[1] = lax.optimization_barrier((own[3], others[1]))
        gathered.append((own, [to_core(value) for value in own]))

    rows_in, rows_out = basis_in.shape[0], basis_out.shape[0]
    rows = ((0, rows_in), (0, rows_out))
    total = None
    for chain in range(CHAINS - 1):
        total = rotate(part, near_at, chain, sum(gathered[chain], []), (basis_in, basis_out), rows, total)
    partial, sent = rotate(part, near_at, CHAINS - 1, sum(gathered[-1], []), bases, rows, total)
    to_sum = [(p * count + i, (1 - p) * count + i) for p in range(2) for i in range(count) if i % 2 != p]
    to_half = [(p * count + i, p * count + (i ^ 1)) for p in range(2) for i in range(count) if i % 2 == p]
    own_tokens = features_of(part, chip_at, *after((acts, grads), sent), [(0, chips)])
    last_piece = give_away(2, sent)
    arrived, last_piece = lax.optimization_barrier((lax.ppermute(sent, EVERYONE, to_sum), last_piece))
    others.append(lax.ppermute(last_piece, EVERYONE, across))
    summed = (partial + arrived.astype(jnp.float32)).astype(jnp.bfloat16)
    given = lax.ppermute(summed[ranks:], EVERYONE, to_half)
    piece = jnp.where(core == part, summed[:ranks], given)

    held = [piece[None]]
    for bit in range(2, bits):
        held.append(to_chip(held[0] if len(held) == 1 else jnp.concatenate(held, axis=0), 1 << bit))
    held[1], *own_tokens = lax.optimization_barrier((held[1], *own_tokens))
    own, sib = [], []
    for source in held:
        group = near_gather(source)
        swapped = [to_core(value) for value in group]
        for step in range(NEAR):
            own += [group[step][entry] for entry in range(source.shape[0])]
            sib += [swapped[SIBLING[step]][entry] for entry in range(source.shape[0])]

    theirs = project(own, sib, rows_in, others, pieces, jnp.bfloat16)
    back = lax.ppermute(jnp.stack(theirs), EVERYONE, across).astype(jnp.float32)
    mine = project(own, sib, rows_in, own_tokens, [(0, chips)], jnp.float32)
    mine_in, mine_out = mine[0] + back[0], mine[1] + back[1]
    seqs = me * seqs_here + jnp.arange(seqs_here, dtype=jnp.int32)
    live = jnp.arange(max_length, dtype=jnp.int32)[None, :] < lengths[slot_plan[seqs]][:, None]
    products = (mine_in * mine_out).reshape(seqs_here, max_length, -1)
    sums = jnp.sum(jnp.where(live[:, :, None], products, 0.0), axis=1)
    held = (jnp.sum(sums.reshape(seqs_here, 2, num_queries, half_rank), axis=(1, 3)) / rank_count)[None]
    for bit in range(bits + 1):
        pairs = [(i, i ^ (1 << bit)) for i in range(count)]
        held = jnp.concatenate([held, lax.ppermute(held, "blk", pairs)], axis=0)
    from_device = jnp.arange(count, dtype=jnp.int32) ^ me
    planned = slot_plan.reshape(count, seqs_here)[from_device]
    chooser = planned[None, :, :] == seqs[:, None, None]
    return jnp.sum(jnp.where(chooser[..., None], held[None], 0.0), axis=(1, 2))


def solution(mesh):
    placed = (
        P(("parts", "blk"), None, None),
        P(("parts", "blk"), None, None),
        P("blk", None),
        P("blk", None),
        P("blk", None, None),
        P("blk", None, None),
        P(),
        P("parts"),
        P("parts"),
    )
    return jax.shard_map(
        shards, mesh=mesh, in_specs=placed, out_specs=P(("parts", "blk"), None), check_vma=False
    )
```

```python
import jax
import jax.numpy as jnp
from jax import lax
from jax.experimental import pallas as pl
from jax.experimental.pallas import tpu as pltpu
from jax.sharding import PartitionSpec as P

ROWS = (((1,), (1,)), ((), ()))
EVERYONE = ("parts", "blk")
NEAR = 4
CHAINS = 2
SHARES = (3, 2, 3)
MIB = 1024 * 1024


def dot_rows(left, right):
    return lax.dot_general(left, right, ROWS, preferred_element_type=jnp.float32)


NEAR_MASKS = ((0, 1, 2, 3), (0, 2, 1, 3))
SIBLING = (0, 2, 1, 3)


def after(values, other):
    return list(lax.optimization_barrier((*values, other)))[:-1]


VMEM = pl.BlockSpec(memory_space=pltpu.VMEM)
SMEM = pl.BlockSpec(memory_space=pltpu.SMEM)
HBM = pl.BlockSpec(memory_space=pltpu.HBM)


def in_hbm(value):
    return pltpu.with_memory_space_constraint(value, pltpu.HBM)


def in_vmem(value):
    return pltpu.with_memory_space_constraint(value, pltpu.VMEM)


def lanes_at(number, width):
    return pl.ds(pl.multiple_of(number * width, 128), width)


def copy_all(copies):
    for copy in copies:
        copy.start()
    for copy in copies:
        copy.wait()


def estimate(flops, moved):
    return pl.CostEstimate(flops=flops, bytes_accessed=moved, transcendentals=0)


def rank_halves(part, core, left, right):
    half_rank = left.shape[1] // 2
    widths = [factor.shape[2] // (2 * CHAINS * NEAR) for factor in (left, right)]
    wide = sum(widths)

    def kernel(where, left, right, away, kept, sems):
        copies = []
        for side, out in enumerate((away, kept)):
            rows = pl.ds(pl.multiple_of((where[1] if side else 1 - where[1]) * half_rank, half_rank), half_rank)
            for chunk in range(NEAR):
                for chain in range(CHAINS):
                    number = (where[0] * CHAINS + chain) * NEAR + chunk
                    target = out.at[chunk, chain]
                    copies.append(
                        pltpu.make_async_copy(
                            left.at[0, rows, lanes_at(number, widths[0])],
                            target.at[:, pl.ds(0, widths[0])],
                            sems.at[len(copies)],
                        )
                    )
                    copies.append(
                        pltpu.make_async_copy(
                            right.at[0, rows, lanes_at(number, widths[1])],
                            target.at[:, pl.ds(widths[0], widths[1])],
                            sems.at[len(copies)],
                        )
                    )
        copy_all(copies)

    shape = (NEAR, CHAINS, half_rank, wide)
    return pl.pallas_call(
        kernel,
        in_specs=[SMEM, HBM, HBM],
        out_specs=[VMEM] * 2,
        out_shape=[pltpu.VMEM(shape, left.dtype)] * 2,
        scratch_shapes=[pltpu.SemaphoreType.DMA((4 * NEAR * CHAINS,))],
        compiler_params=pltpu.CompilerParams(vmem_limit_bytes=4 * MIB),
        cost_estimate=estimate(0, 8 * NEAR * CHAINS * half_rank * wide),
        name="rank_halves",
    )(jnp.stack([part, core]), in_hbm(left), in_hbm(right))


def messages_of(spot, kept, received):
    def kernel(where, kept, received, *outs):
        for chain in range(CHAINS):
            for mask in range(NEAR):
                chunk = where[0] ^ mask
                outs[chain * NEAR + mask][0] = kept[chunk, chain]
                outs[chain * NEAR + mask][1] = received[chunk, chain]

    shape = jax.ShapeDtypeStruct((2,) + kept.shape[2:], kept.dtype)
    outs = pl.pallas_call(
        kernel,
        in_specs=[SMEM, VMEM, VMEM],
        out_specs=[VMEM] * (NEAR * CHAINS),
        out_shape=[shape] * (NEAR * CHAINS),
        compiler_params=pltpu.CompilerParams(vmem_limit_bytes=4 * MIB),
        cost_estimate=estimate(0, 4 * 2 * kept.size),
        name="messages",
    )(spot[None], kept, received)
    return [outs[chain * NEAR : (chain + 1) * NEAR] for chain in range(CHAINS)]


def stage_bases(part, bases):
    widths = [basis.shape[1] // 2 for basis in bases]

    def kernel(where, first, second, first_out, second_out, sems):
        copies = []
        for num, (basis, out, shape) in enumerate(((first, first_out, shapes[0]), (second, second_out, shapes[1]))):
            copies.append(pltpu.make_async_copy(basis.at[:, lanes_at(where[0], shape[1])], out, sems.at[num]))
        copy_all(copies)

    shapes = [(basis.shape[0], width) for basis, width in zip(bases, widths)]
    return pl.pallas_call(
        kernel,
        in_specs=[SMEM, HBM, HBM],
        out_specs=[VMEM] * 2,
        out_shape=[pltpu.VMEM(shape, bases[0].dtype) for shape in shapes],
        scratch_shapes=[pltpu.SemaphoreType.DMA((2,))],
        compiler_params=pltpu.CompilerParams(vmem_limit_bytes=4 * MIB),
        cost_estimate=estimate(0, 2 * sum(shape[0] * shape[1] for shape in shapes)),
        name="stage_bases",
    )(part[None], *map(in_hbm, bases))


def choose(spot, found):
    queries = spot.shape[0]
    ranks, wide = found[0].shape[1:]

    def kernel(where, *rest):
        out = rest[-1]
        for query in range(queries):
            place = pl.ds(query * ranks, ranks)
            for mask in range(NEAR):

                @pl.when(where[query] // 2 == mask)
                def _():
                    out[0, place] = rest[mask][where[query] % 2]

            @pl.when(where[query] >= 2 * NEAR)
            def _():
                out[0, place] = jnp.zeros((ranks, wide), out.dtype)

    return pl.pallas_call(
        kernel,
        in_specs=[SMEM] + [VMEM] * NEAR,
        out_specs=VMEM,
        out_shape=jax.ShapeDtypeStruct((1, queries * ranks, wide), found[0].dtype),
        compiler_params=pltpu.CompilerParams(vmem_limit_bytes=4 * MIB),
        cost_estimate=estimate(0, 4 * queries * ranks * wide),
        name="choose",
    )(spot, *found)


def features_of(part, chip_at, acts, grads, pieces):
    tokens, chips = acts.shape[0], chip_at.shape[0]
    wide_in, wide_out = acts.shape[1] // 2 // chips, grads.shape[1] // 2 // chips
    wide = wide_in + wide_out
    if wide_in % 128 or wide_out % 128:
        some_in = jnp.take(jnp.take(acts.reshape(tokens, chips, 2, wide_in), part, axis=2), chip_at, axis=1)
        some_out = jnp.take(jnp.take(grads.reshape(tokens, chips, 2, wide_out), part, axis=2), chip_at, axis=1)
        some = jnp.concatenate([some_in, some_out], axis=2)
        return [some[:, begin:end].reshape(tokens, -1) for begin, end in pieces]
    total = sum(end - begin for begin, end in pieces)

    def kernel(where, acts, grads, *rest):
        outs, sems = rest[:-1], rest[-1]
        copies = []
        for out, (first, last) in zip(outs, pieces):
            for spot in range(first, last):
                number = 2 * where[1 + spot] + where[0]
                for source, width, begin in ((acts, wide_in, 0), (grads, wide_out, wide_in)):
                    copies.append(
                        pltpu.make_async_copy(
                            source.at[:, lanes_at(number, width)],
                            out.at[:, pl.ds((spot - first) * wide + begin, width)],
                            sems.at[len(copies)],
                        )
                    )
        copy_all(copies)

    return pl.pallas_call(
        kernel,
        in_specs=[SMEM, HBM, HBM],
        out_specs=[VMEM] * len(pieces),
        out_shape=[pltpu.VMEM((tokens, (end - begin) * wide), acts.dtype) for begin, end in pieces],
        scratch_shapes=[pltpu.SemaphoreType.DMA((2 * total,))],
        compiler_params=pltpu.CompilerParams(vmem_limit_bytes=4 * MIB),
        cost_estimate=estimate(0, 4 * tokens * total * wide),
        name="features",
    )(jnp.concatenate([part[None], chip_at]), in_hbm(acts), in_hbm(grads))


def rotate(chunks, chain, own, sib, bases, total):
    last = chain == CHAINS - 1
    ranks, wide = own[0].shape
    wide_in = bases[0].shape[1] // (CHAINS * NEAR)
    widths = (wide_in, wide - wide_in)
    rows_in = bases[0].shape[0]
    height = rows_in + bases[1].shape[0]
    spans = ((0, rows_in, 0, wide_in), (rows_in, height, wide_in, wide))

    def kernel(where, *rest):
        own_here, sib_here, bases_here, rest = rest[:NEAR], rest[NEAR : 2 * NEAR], rest[2 * NEAR :][:2], rest[2 * NEAR + 2 :]
        if total is not None:
            start, rest = rest[0], rest[1:]
        outs, acc = rest[:-1], rest[-1]
        for spot in range(NEAR):
            factor = jnp.concatenate([own_here[spot][...], sib_here[SIBLING[spot]][...]], axis=0)
            for num, (from_row, to_row, from_lane, to_lane) in enumerate(spans):
                block = bases_here[num][:, lanes_at(chain * NEAR + where[spot], widths[num])]
                value = dot_rows(block, factor[:, from_lane:to_lane])
                if spot:
                    value = value + acc[from_row:to_row]
                elif total is not None:
                    value = value + start[from_row:to_row]
                acc[from_row:to_row] = value
        value = acc[...]
        if last:
            value = value.T
            outs[1][...] = value.astype(jnp.bfloat16)
        outs[0][...] = value

    if last:
        shapes = [jax.ShapeDtypeStruct((2 * ranks, height), kind) for kind in (jnp.float32, jnp.bfloat16)]
    else:
        shapes = [jax.ShapeDtypeStruct((height, 2 * ranks), jnp.float32)]
    given = [] if total is None else [total]
    moved = sum((to_row - from_row) * (to_lane - from_lane) for from_row, to_row, from_lane, to_lane in spans)
    results = pl.pallas_call(
        kernel,
        in_specs=[SMEM] + [VMEM] * (2 * NEAR + 2 + len(given)),
        out_specs=[VMEM] * len(shapes),
        out_shape=shapes,
        scratch_shapes=[pltpu.VMEM((height, 2 * ranks), jnp.float32)],
        compiler_params=pltpu.CompilerParams(vmem_limit_bytes=4 * MIB),
        cost_estimate=estimate(4 * ranks * NEAR * moved, 2 * NEAR * moved),
        name="rotate",
    )(chunks, *own, *sib, *map(in_vmem, bases), *given)
    return tuple(results) if last else results[0]


def project(own, sib, wide_in, tokens_in, pieces, kind):
    chips = len(own)
    ranks, wide = own[0].shape
    tokens = tokens_in[0].shape[0]
    if wide_in % 128 or wide % 128:
        both = jnp.stack([jnp.concatenate(pair, axis=0) for pair in zip(own, sib)])
        held = jnp.concatenate(tokens_in, axis=1).reshape(tokens, chips, wide)
        return [
            jnp.einsum("tgf,gcf->tc", held[:, :, lanes], both[:, :, lanes], preferred_element_type=jnp.float32).astype(
                kind
            )
            for lanes in (slice(0, wide_in), slice(wide_in, wide))
        ]

    def kernel(*rest):
        factors, rest = rest[: 2 * chips], rest[2 * chips :]
        held, rest = rest[: len(tokens_in)], rest[len(tokens_in) :]
        outs, acc = rest[:2], rest[2]
        for source, (first, last) in zip(held, pieces):
            for spot in range(first, last):
                factor = jnp.concatenate([factors[spot][...], factors[chips + spot][...]], axis=0)
                for num, (begin, end) in enumerate(((0, wide_in), (wide_in, wide))):
                    base = (spot - first) * wide
                    value = dot_rows(source[:, base + begin : base + end], factor[:, begin:end])
                    acc[num] = value if spot == 0 else acc[num] + value
        for num, out in enumerate(outs):
            out[...] = acc[num].astype(kind)

    return pl.pallas_call(
        kernel,
        in_specs=[VMEM] * (2 * chips + len(tokens_in)),
        out_specs=[VMEM] * 2,
        out_shape=[jax.ShapeDtypeStruct((tokens, 2 * ranks), kind)] * 2,
        scratch_shapes=[pltpu.VMEM((2, tokens, 2 * ranks), jnp.float32)],
        compiler_params=pltpu.CompilerParams(vmem_limit_bytes=4 * MIB),
        cost_estimate=estimate(4 * tokens * ranks * chips * wide, 4 * ranks * chips * wide),
        name="project",
    )(*own, *sib, *map(in_vmem, tokens_in))


def score(me, lengths, slot_plan, mine, back, queries, rank_count):
    tokens, columns = mine[0].shape
    half_rank = rank_count // 2
    lanes = slot_plan.shape[0] * queries

    def kernel(where, lengths, slot_plan, mine_in, mine_out, back, out):
        live = lax.broadcasted_iota(jnp.int32, (tokens, columns), 0) < lengths[slot_plan[where[0]]]
        products = (mine_in[...] + back[0].astype(jnp.float32)) * (mine_out[...] + back[1].astype(jnp.float32))
        sums = jnp.sum(jnp.where(live, products, 0.0), axis=0, keepdims=True)
        query_of = lax.broadcasted_iota(jnp.int32, (1, columns), 1) % (queries * half_rank) // half_rank
        lane = lax.broadcasted_iota(jnp.int32, (1, lanes), 1)
        row = jnp.zeros((1, lanes), jnp.float32)
        for query in range(queries):
            value = jnp.sum(jnp.where(query_of == query, sums, 0.0), axis=1, keepdims=True) / rank_count
            row = jnp.where(lane == where[0] * queries + query, value, row)
        out[...] = row

    return pl.pallas_call(
        kernel,
        in_specs=[SMEM] * 3 + [VMEM] * 3,
        out_specs=VMEM,
        out_shape=jax.ShapeDtypeStruct((1, lanes), jnp.float32),
        compiler_params=pltpu.CompilerParams(vmem_limit_bytes=4 * MIB),
        cost_estimate=estimate(6 * tokens * columns, 12 * tokens * columns),
        name="score",
    )(me[None], lengths, slot_plan, *mine, back)


def own_sequence(me, slot_plan, held, queries):
    slots = slot_plan.shape[0]

    def kernel(where, slot_plan, held, out):
        slot = jnp.int32(0)
        for number in range(slots):
            slot = jnp.where(slot_plan[number] == where[0], number, slot)
        lane = lax.broadcasted_iota(jnp.int32, held.shape, 1)
        out_lane = lax.broadcasted_iota(jnp.int32, (1, queries), 1)
        row = jnp.zeros((1, queries), jnp.float32)
        for query in range(queries):
            value = jnp.sum(jnp.where(lane == slot * queries + query, held[...], 0.0), axis=1, keepdims=True)
            row = jnp.where(out_lane == query, value, row)
        out[...] = row

    return pl.pallas_call(
        kernel,
        in_specs=[SMEM] * 2 + [VMEM],
        out_specs=VMEM,
        out_shape=jax.ShapeDtypeStruct((1, queries), jnp.float32),
        compiler_params=pltpu.CompilerParams(vmem_limit_bytes=4 * MIB),
        cost_estimate=estimate(0, 4 * held.size),
        name="own_sequence",
    )(me[None], slot_plan, held)


def shards(
    activations,
    output_grads,
    basis_in,
    basis_out,
    query_left,
    query_right,
    owners,
    lengths,
    slot_plan,
):
    count = lax.axis_size("blk")
    chips = count // 2
    bits = chips.bit_length() - 1
    me = lax.axis_index("blk")
    part = lax.axis_index("parts")
    core, chip = me % 2, me // 2
    seqs_here, max_length, width_in = activations.shape
    num_queries = owners.shape[0]
    rank_count = query_left.shape[1]
    half_rank = rank_count // 2
    ranks = num_queries * half_rank
    tokens = seqs_here * max_length
    acts = activations.reshape(tokens, width_in)
    grads = output_grads.reshape(tokens, -1)
    across = [(p * count + i, (1 - p) * count + i) for p in range(2) for i in range(count)]

    def to_chip(value, mask):
        return lax.ppermute(value, "blk", [(i, i ^ (2 * mask)) for i in range(count)])

    def along(value, first, second):
        return lax.ppermute(value, "blk", [(i, i ^ (2 << (second if i % 2 else first))) for i in range(count)])

    def to_core(value):
        return lax.ppermute(value, "blk", [(i, i ^ 1) for i in range(count)])

    def near_gather(value):
        first = along(value, 0, 1)
        second = along(value, 1, 0)
        return [value, first, second, along(first, 1, 0)]

    near_at = jnp.where(core == 0, jnp.array(NEAR_MASKS[0], jnp.int32), jnp.array(NEAR_MASKS[1], jnp.int32)) ^ (
        chip % NEAR
    )
    sources = [[0]]
    for bit in range(2, bits):
        sources.append([mask | (1 << bit) for group in sources for mask in group])
    orders = [[far | near for group in sources for near in NEAR_MASKS[side] for far in group] for side in range(2)]
    chip_at = jnp.where(core == 0, jnp.array(orders[0], jnp.int32), jnp.array(orders[1], jnp.int32)) ^ chip

    away, kept = rank_halves(part, core, query_left, query_right)
    messages = messages_of(chip % NEAR, kept, to_core(away))
    shares = [chips * sum(SHARES[:num]) // sum(SHARES) for num in range(len(SHARES) + 1)]
    pieces = list(zip(shares[:-1], shares[1:]))

    def give_away(num, other):
        (piece,) = features_of(1 - part, chip_at, *after((acts, grads), other), pieces[num : num + 1])
        return piece

    others = [lax.ppermute(give_away(0, messages[0][0]), EVERYONE, across)]

    source = (owners // 2) ^ chip
    spot = jnp.where(source < NEAR, source * 2 + ((owners % 2) ^ core), 2 * NEAR)
    every = range(CHAINS)
    found = [[to_chip(group[mask], mask) if mask else group[0] for mask in range(NEAR)] for group in messages]
    dense = []
    for chain in every:
        if chain:
            found[chain] = after(found[chain], dense[chain - 1])
        dense.append(choose(spot, found[chain]))
        if chain == 0:
            second = give_away(1, dense[0])
            found[1][0], second = lax.optimization_barrier((found[1][0], second))
    others = [others[0], lax.ppermute(second, EVERYONE, across)]
    bases = stage_bases(part, after((basis_in, basis_out), dense[-1]))
    for bit in range(bits - 1, 1, -1):
        arrived = [to_chip(dense[chain], 1 << bit) for chain in every]
        if bit == bits - 1:
            others[0], arrived[0], *bases = lax.optimization_barrier((others[0], arrived[0], *bases))
        for chain in every:
            if chain:
                (arrived[chain],) = after((arrived[chain],), dense[chain - 1])
            dense[chain] = dense[chain] + arrived[chain]
    total = None
    for chain in every:
        own = near_gather(dense[chain][0])
        if chain:
            own[1:3] = after(own[1:3], first)
            (own[3],) = after((own[3],), total)
        first = own[1]
        total = rotate(near_at, chain, own, [to_core(value) for value in own], bases, total)

    partial, sent = total
    to_sum = [(p * count + i, (1 - p) * count + i) for p in range(2) for i in range(count) if i % 2 != p]
    to_half = [(p * count + i, p * count + (i ^ 1)) for p in range(2) for i in range(count) if i % 2 == p]
    own_tokens = features_of(part, chip_at, *after((acts, grads), sent), [(0, chips)])
    last_piece = give_away(2, sent)
    arrived, others[1], last_piece = lax.optimization_barrier((lax.ppermute(sent, EVERYONE, to_sum), others[1], last_piece))
    others.append(lax.ppermute(last_piece, EVERYONE, across))
    summed = (partial + arrived.astype(jnp.float32)).astype(jnp.bfloat16)
    given = lax.ppermute(summed[ranks:], EVERYONE, to_half)
    piece = jnp.where(core == part, summed[:ranks], given)

    held = [piece[None]]
    for bit in range(2, bits):
        held.append(to_chip(held[0] if len(held) == 1 else jnp.concatenate(held, axis=0), 1 << bit))
    held[1], *own_tokens = lax.optimization_barrier((held[1], *own_tokens))
    own, sib = [], []
    for source in held:
        group = near_gather(source)
        swapped = [to_core(value) for value in group]
        for step in range(NEAR):
            own += [group[step][entry] for entry in range(source.shape[0])]
            sib += [swapped[SIBLING[step]][entry] for entry in range(source.shape[0])]

    theirs = project(own, sib, basis_in.shape[0], others, pieces, jnp.bfloat16)
    back = lax.ppermute(jnp.stack(theirs), EVERYONE, across)
    mine = project(own, sib, basis_in.shape[0], own_tokens, [(0, chips)], jnp.float32)

    held = score(me, lengths, slot_plan, mine, back, num_queries, rank_count)
    for bit in range(bits + 1):
        held = held + lax.ppermute(held, "blk", [(i, i ^ (1 << bit)) for i in range(count)])
    return own_sequence(me, slot_plan, held, num_queries)


def solution(mesh):
    placed = (
        P(("parts", "blk"), None, None),
        P(("parts", "blk"), None, None),
        P("blk", None),
        P("blk", None),
        P("blk", None, None),
        P("blk", None, None),
        P(),
        P("parts"),
        P("parts"),
    )
    return jax.shard_map(
        shards, mesh=mesh, in_specs=placed, out_specs=P(("parts", "blk"), None), check_vma=False
    )
```

```python
import jax
import jax.numpy as jnp
from jax import lax
from jax.experimental import pallas as pl
from jax.experimental.pallas import tpu as pltpu
from jax.sharding import PartitionSpec as P

ROWS = (((1,), (1,)), ((), ()))
EVERYONE = ("parts", "blk")
NEAR = 4
CHAINS = 2
PART, CORE, CHIP, ME, NEAR_AT, CHIP_AT = 0, 1, 2, 3, 4, 8
MIB = 1024 * 1024


def dot_rows(left, right):
    return lax.dot_general(left, right, ROWS, preferred_element_type=jnp.float32)


NEAR_MASKS = ((0, 1, 2, 3), (0, 2, 1, 3))
SIBLING = (0, 2, 1, 3)


def after(values, other):
    return list(lax.optimization_barrier((*values, other)))[:-1]


VMEM = pl.BlockSpec(memory_space=pltpu.VMEM)
SMEM = pl.BlockSpec(memory_space=pltpu.SMEM)
HBM = pl.BlockSpec(memory_space=pltpu.HBM)


def in_hbm(value):
    return pltpu.with_memory_space_constraint(value, pltpu.HBM)


def in_vmem(value):
    return pltpu.with_memory_space_constraint(value, pltpu.VMEM)


def lanes_at(number, width):
    return pl.ds(pl.multiple_of(number * width, 128), width)


def copy_all(copies):
    for copy in copies:
        copy.start()
    for copy in copies:
        copy.wait()


def estimate(flops, moved):
    return pl.CostEstimate(flops=flops, bytes_accessed=moved, transcendentals=0)


class Features:
    def __init__(self, acts, grads, chips):
        self.tokens, self.chips, self.kind = acts.shape[0], chips, acts.dtype
        self.acts, self.grads = acts, grads
        self.wide_in, self.wide_out = acts.shape[1] // 2 // chips, grads.shape[1] // 2 // chips
        self.wide = self.wide_in + self.wide_out
        self.aligned = not (self.wide_in % 128 or self.wide_out % 128)

    def shapes(self, ranges):
        return [pltpu.VMEM((self.tokens, (end - begin) * self.wide), self.kind) for begin, end in ranges]

    def copies(self, sources, outs, ranges, plane, chip_at, sems):
        result = []
        for out, (first, last) in zip(outs, ranges):
            for spot in range(first, last):
                number = 2 * chip_at(spot) + plane
                for source, width, begin in zip(sources, (self.wide_in, self.wide_out), (0, self.wide_in)):
                    result.append(
                        pltpu.make_async_copy(
                            source.at[:, lanes_at(number, width)],
                            out.at[:, pl.ds((spot - first) * self.wide + begin, width)],
                            sems.at[len(result)],
                        )
                    )
        return result

    def plain(self, ranges, plane, chip_at):
        some = [
            jnp.take(jnp.take(value.reshape(self.tokens, self.chips, 2, width), plane, axis=2), chip_at, axis=1)
            for value, width in ((self.acts, self.wide_in), (self.grads, self.wide_out))
        ]
        some = jnp.concatenate(some, axis=2)
        return [some[:, begin:end].reshape(self.tokens, -1) for begin, end in ranges]


def rank_halves(info, left, right):
    half_rank = left.shape[1] // 2
    widths = [factor.shape[2] // (2 * CHAINS * NEAR) for factor in (left, right)]
    wide = sum(widths)

    def kernel(where, left, right, away, kept, sems):
        copies = []
        for side, out in enumerate((away, kept)):
            half = where[CORE] if side else 1 - where[CORE]
            rows = pl.ds(pl.multiple_of(half * half_rank, half_rank), half_rank)
            for chunk in range(NEAR):
                for chain in range(CHAINS):
                    number = (where[PART] * CHAINS + chain) * NEAR + chunk
                    for source, width, begin in zip((left, right), widths, (0, widths[0])):
                        copies.append(
                            pltpu.make_async_copy(
                                source.at[0, rows, lanes_at(number, width)],
                                out.at[chunk, chain, :, pl.ds(begin, width)],
                                sems.at[len(copies)],
                            )
                        )
        copy_all(copies)

    shape = (NEAR, CHAINS, half_rank, wide)
    return pl.pallas_call(
        kernel,
        in_specs=[SMEM] + [HBM] * 2,
        out_specs=[VMEM] * 2,
        out_shape=[pltpu.VMEM(shape, left.dtype)] * 2,
        scratch_shapes=[pltpu.SemaphoreType.DMA((4 * NEAR * CHAINS,))],
        compiler_params=pltpu.CompilerParams(vmem_limit_bytes=4 * MIB),
        cost_estimate=estimate(0, 8 * NEAR * CHAINS * half_rank * wide),
        name="rank_halves",
    )(info, in_hbm(left), in_hbm(right))


def messages_of(info, kept, received):
    def kernel(where, kept, received, *outs):
        for mask, out in enumerate(outs):
            chunk = (where[CHIP] % NEAR) ^ mask
            out[0] = kept[chunk]
            out[1] = received[chunk]

    shape = jax.ShapeDtypeStruct((2,) + kept.shape[1:], kept.dtype)
    return pl.pallas_call(
        kernel,
        in_specs=[SMEM, VMEM, VMEM],
        out_specs=[VMEM] * NEAR,
        out_shape=[shape] * NEAR,
        compiler_params=pltpu.CompilerParams(vmem_limit_bytes=4 * MIB),
        cost_estimate=estimate(0, 4 * 2 * kept.size),
        name="messages",
    )(info, kept, received)


def stage(info, bases, features, given, kept):
    shapes = [(basis.shape[0], basis.shape[1] // 2) for basis in bases]
    ranges = given + kept if features.aligned else []
    total = sum(end - begin for begin, end in ranges)
    plain = []
    if not features.aligned:
        chip_at = info[CHIP_AT : CHIP_AT + features.chips]
        plain = features.plain(given, 1 - info[PART], chip_at) + features.plain(kept, info[PART], chip_at)
        if not bases:
            return plain

    def kernel(where, acts, grads, *rest):
        sources, outs, (sems, more) = rest[: len(bases)], rest[len(bases) : -2], rest[-2:]
        copies = []
        moved = 0
        for num, out in enumerate(outs[len(bases) :]):
            plane = 1 - where[PART] if num < len(given) else where[PART]
            count = 2 * (ranges[num][1] - ranges[num][0])
            copies += features.copies(
                (acts, grads),
                [out],
                ranges[num : num + 1],
                plane,
                lambda spot: where[CHIP_AT + spot],
                more.at[pl.ds(moved, count)],
            )
            moved += count
        for num, (basis, shape) in enumerate(zip(sources, shapes)):
            copies.append(pltpu.make_async_copy(basis.at[:, lanes_at(where[PART], shape[1])], outs[num], sems.at[num]))
        copy_all(copies)

    results = pl.pallas_call(
        kernel,
        in_specs=[SMEM] + [HBM] * (2 + len(bases)),
        out_specs=[VMEM] * (len(bases) + len(ranges)),
        out_shape=[pltpu.VMEM(shape, features.kind) for shape in shapes] + features.shapes(ranges),
        scratch_shapes=[pltpu.SemaphoreType.DMA((2,)), pltpu.SemaphoreType.DMA((max(2 * total, 1),))],
        compiler_params=pltpu.CompilerParams(vmem_limit_bytes=4 * MIB),
        cost_estimate=estimate(0, 2 * sum(shape[0] * shape[1] for shape in shapes)),
        name="stage",
    )(info, *map(in_hbm, (features.acts, features.grads, *bases)))
    return list(results) + plain


def choose(info, queries, found):
    ranks, wide = found[0].shape[2:]
    chips = (info.shape[0] - CHIP_AT - queries) // 5

    def kernel(where, *rest):
        outs = rest[NEAR:]
        for query in range(queries):
            owner = where[CHIP_AT + chips + query]
            place = pl.ds(query * ranks, ranks)
            mask_of = (owner // 2) ^ where[CHIP]
            side = (owner % 2) ^ where[CORE]
            for chain, out in enumerate(outs):
                for mask in range(NEAR):

                    @pl.when(mask_of == mask)
                    def _():
                        out[place] = rest[mask][side, chain]

                @pl.when(mask_of >= NEAR)
                def _():
                    out[place] = jnp.zeros((ranks, wide), out.dtype)

    return pl.pallas_call(
        kernel,
        in_specs=[SMEM] + [VMEM] * NEAR,
        out_specs=[VMEM] * CHAINS,
        out_shape=[jax.ShapeDtypeStruct((queries * ranks, wide), found[0].dtype)] * CHAINS,
        compiler_params=pltpu.CompilerParams(vmem_limit_bytes=4 * MIB),
        cost_estimate=estimate(0, 4 * queries * ranks * wide * CHAINS),
        name="choose",
    )(info, *found)


def meet_halves(info, partial, met, crossed):
    def kernel(where, partial, met, crossed, out):
        @pl.when(where[CORE] == where[PART])
        def _():
            out[...] = (partial[...] + met[...].astype(jnp.float32)).astype(out.dtype)

        @pl.when(where[CORE] != where[PART])
        def _():
            out[...] = (crossed[...].astype(jnp.float32) + met[...].astype(jnp.float32)).astype(out.dtype)

    return pl.pallas_call(
        kernel,
        in_specs=[SMEM] + [VMEM] * 3,
        out_specs=VMEM,
        out_shape=jax.ShapeDtypeStruct(met.shape, met.dtype),
        compiler_params=pltpu.CompilerParams(vmem_limit_bytes=4 * MIB),
        cost_estimate=estimate(2 * partial.size, 10 * partial.size),
        name="meet_halves",
    )(info, partial, met, crossed)


def rotate(info, chain, own, sib, bases, total):
    last = chain == CHAINS - 1
    ranks, wide = own[0].shape
    wide_in = bases[0].shape[1] // (CHAINS * NEAR)
    widths = (wide_in, wide - wide_in)
    rows_in = bases[0].shape[0]
    height = rows_in + bases[1].shape[0]
    spans = ((0, rows_in, 0, wide_in), (rows_in, height, wide_in, wide))

    def kernel(where, *rest):
        own_here, sib_here, bases_here, rest = rest[:NEAR], rest[NEAR : 2 * NEAR], rest[2 * NEAR :][:2], rest[2 * NEAR + 2 :]
        if total is not None:
            start, rest = rest[0], rest[1:]
        outs, acc = rest[:-1], rest[-1]
        for spot in range(NEAR):
            factor = jnp.concatenate([own_here[spot][...], sib_here[SIBLING[spot]][...]], axis=0)
            for num, (from_row, to_row, from_lane, to_lane) in enumerate(spans):
                block = bases_here[num][:, lanes_at(chain * NEAR + where[NEAR_AT + spot], widths[num])]
                value = dot_rows(block, factor[:, from_lane:to_lane])
                if spot:
                    value = value + acc[from_row:to_row]
                elif total is not None:
                    value = value + start[from_row:to_row]
                acc[from_row:to_row] = value
        if last:
            value = acc[...].T
            outs[0][...] = value[:ranks]
            outs[1][...] = jnp.where(where[CORE] == where[PART], value[ranks:], value[:ranks]).astype(jnp.bfloat16)
            outs[2][...] = value[ranks:].astype(jnp.bfloat16)
        else:
            outs[0][...] = acc[...]

    if last:
        shapes = [jax.ShapeDtypeStruct((ranks, height), kind) for kind in (jnp.float32, jnp.bfloat16, jnp.bfloat16)]
    else:
        shapes = [jax.ShapeDtypeStruct((height, 2 * ranks), jnp.float32)]
    given = [] if total is None else [total]
    moved = sum((to_row - from_row) * (to_lane - from_lane) for from_row, to_row, from_lane, to_lane in spans)
    results = pl.pallas_call(
        kernel,
        in_specs=[SMEM] + [VMEM] * (2 * NEAR + 2 + len(given)),
        out_specs=[VMEM] * len(shapes),
        out_shape=shapes,
        scratch_shapes=[pltpu.VMEM((height, 2 * ranks), jnp.float32)],
        compiler_params=pltpu.CompilerParams(vmem_limit_bytes=4 * MIB),
        cost_estimate=estimate(4 * ranks * NEAR * moved, 2 * NEAR * moved),
        name="rotate",
    )(info, *own, *sib, *map(in_vmem, bases), *given)
    return tuple(results) if last else results[0]


def project(arrays, own, sib, wide_in, tokens_in, pieces, kind):
    chips = len(own)
    ranks, wide = arrays[0].shape[1:]
    tokens = tokens_in[0].shape[0]
    if wide_in % 128 or wide % 128:
        both = jnp.stack([jnp.concatenate([arrays[i][m], arrays[j][n]], axis=0) for (i, m), (j, n) in zip(own, sib)])
        held = jnp.concatenate(tokens_in, axis=1).reshape(tokens, chips, wide)
        return [
            jnp.einsum("tgf,gcf->tc", held[:, :, lanes], both[:, :, lanes], preferred_element_type=jnp.float32).astype(
                kind
            )
            for lanes in (slice(0, wide_in), slice(wide_in, wide))
        ]

    def kernel(*rest):
        factors, rest = rest[: len(arrays)], rest[len(arrays) :]
        held, rest = rest[: len(tokens_in)], rest[len(tokens_in) :]
        outs, acc = rest[:2], rest[2]
        for source, (first, last) in zip(held, pieces):
            for spot in range(first, last):
                (i, m), (j, n) = own[spot], sib[spot]
                factor = jnp.concatenate([factors[i][m], factors[j][n]], axis=0)
                for num, (begin, end) in enumerate(((0, wide_in), (wide_in, wide))):
                    base = (spot - first) * wide
                    value = dot_rows(source[:, base + begin : base + end], factor[:, begin:end])
                    acc[num] = value if spot == 0 else acc[num] + value
        for num, out in enumerate(outs):
            out[...] = acc[num].astype(kind)

    return pl.pallas_call(
        kernel,
        in_specs=[VMEM] * (len(arrays) + len(tokens_in)),
        out_specs=[VMEM] * 2,
        out_shape=[jax.ShapeDtypeStruct((tokens, 2 * ranks), kind)] * 2,
        scratch_shapes=[pltpu.VMEM((2, tokens, 2 * ranks), jnp.float32)],
        compiler_params=pltpu.CompilerParams(vmem_limit_bytes=4 * MIB),
        cost_estimate=estimate(4 * tokens * ranks * chips * wide, 4 * ranks * chips * wide),
        name="project",
    )(*arrays, *map(in_vmem, tokens_in))


def score(info, slots, mine, back, queries, rank_count):
    tokens, columns = mine[0].shape
    half_rank = rank_count // 2
    lanes = slots * queries
    lengths_at = info.shape[0] - 2 * slots

    def kernel(where, mine_in, mine_out, back, out):
        live = lax.broadcasted_iota(jnp.int32, (tokens, columns), 0) < where[lengths_at + where[lengths_at + slots + where[ME]]]
        products = (mine_in[...] + back[0].astype(jnp.float32)) * (mine_out[...] + back[1].astype(jnp.float32))
        sums = jnp.sum(jnp.where(live, products, 0.0), axis=0, keepdims=True)
        query_of = lax.broadcasted_iota(jnp.int32, (1, columns), 1) % (queries * half_rank) // half_rank
        lane = lax.broadcasted_iota(jnp.int32, (1, lanes), 1)
        row = jnp.zeros((1, lanes), jnp.float32)
        for query in range(queries):
            value = jnp.sum(jnp.where(query_of == query, sums, 0.0), axis=1, keepdims=True) / rank_count
            row = jnp.where(lane == where[ME] * queries + query, value, row)
        out[...] = row

    return pl.pallas_call(
        kernel,
        in_specs=[SMEM] + [VMEM] * 3,
        out_specs=VMEM,
        out_shape=jax.ShapeDtypeStruct((1, lanes), jnp.float32),
        compiler_params=pltpu.CompilerParams(vmem_limit_bytes=4 * MIB),
        cost_estimate=estimate(6 * tokens * columns, 12 * tokens * columns),
        name="score",
    )(info, *mine, back)


def own_sequence(info, slots, held, queries):
    plan_at = info.shape[0] - slots

    def kernel(where, held, out):
        slot = jnp.int32(0)
        for number in range(slots):
            slot = jnp.where(where[plan_at + number] == where[ME], number, slot)
        lane = lax.broadcasted_iota(jnp.int32, held.shape, 1)
        out_lane = lax.broadcasted_iota(jnp.int32, (1, queries), 1)
        row = jnp.zeros((1, queries), jnp.float32)
        for query in range(queries):
            value = jnp.sum(jnp.where(lane == slot * queries + query, held[...], 0.0), axis=1, keepdims=True)
            row = jnp.where(out_lane == query, value, row)
        out[...] = row

    return pl.pallas_call(
        kernel,
        in_specs=[SMEM, VMEM],
        out_specs=VMEM,
        out_shape=jax.ShapeDtypeStruct((1, queries), jnp.float32),
        compiler_params=pltpu.CompilerParams(vmem_limit_bytes=4 * MIB),
        cost_estimate=estimate(0, 4 * held.size),
        name="own_sequence",
    )(info, held)


def shards(
    activations,
    output_grads,
    basis_in,
    basis_out,
    query_left,
    query_right,
    owners,
    lengths,
    slot_plan,
):
    count = lax.axis_size("blk")
    chips = count // 2
    bits = chips.bit_length() - 1
    me = lax.axis_index("blk")
    part = lax.axis_index("parts")
    core, chip = me % 2, me // 2
    seqs_here, max_length, width_in = activations.shape
    num_queries = owners.shape[0]
    rank_count = query_left.shape[1]
    half_rank = rank_count // 2
    ranks = num_queries * half_rank
    tokens = seqs_here * max_length
    acts = activations.reshape(tokens, width_in)
    grads = output_grads.reshape(tokens, -1)
    across = [(p * count + i, (1 - p) * count + i) for p in range(2) for i in range(count)]

    def to_chip(value, mask):
        return lax.ppermute(value, "blk", [(i, i ^ (2 * mask)) for i in range(count)])

    def along(value, first, second):
        return lax.ppermute(value, "blk", [(i, i ^ (2 << (second if i % 2 else first))) for i in range(count)])

    def to_core(value):
        return lax.ppermute(value, "blk", [(i, i ^ 1) for i in range(count)])

    def near_gather(value, before=None):
        first = along(value, 0, 1)
        if before is not None:
            (first,) = after((first,), before)
        low = jnp.concatenate([value, first], axis=0)
        return low, along(low, 1, 0)

    def near_pieces(value):
        first = along(value, 0, 1)
        second = along(value, 1, 0)
        return [value, first, second, along(first, 1, 0)]

    near_at = jnp.where(core == 0, jnp.array(NEAR_MASKS[0], jnp.int32), jnp.array(NEAR_MASKS[1], jnp.int32)) ^ (
        chip % NEAR
    )
    sources = [[0]]
    for bit in range(2, bits):
        sources.append([mask | (1 << bit) for group in sources for mask in group])
    orders = [[far | near for group in sources for near in NEAR_MASKS[side] for far in group] for side in range(2)]
    chip_at = jnp.where(core == 0, jnp.array(orders[0], jnp.int32), jnp.array(orders[1], jnp.int32)) ^ chip

    (info,) = lax.optimization_barrier((jnp.concatenate([jnp.stack([part, core, chip, me]), near_at, chip_at]),))

    far = (NEAR, chips)

    away, kept = rank_halves(info, query_left, query_right)
    more = jnp.concatenate([info, *after((owners, lengths, slot_plan), away)])
    received, more = lax.optimization_barrier((to_core(away), more))
    messages = messages_of(info, kept, received)

    every = range(CHAINS)
    found = [to_chip(value, mask) if mask else value for mask, value in enumerate(messages)]
    dense = list(choose(more, num_queries, found))
    early = Features(*after((acts, grads), messages[0]), chips)
    (given_away,) = stage(info, [], early, [far], [])
    late = lax.optimization_barrier((acts, grads, basis_in, basis_out, given_away))
    given_away = lax.ppermute(given_away, EVERYONE, across)
    *bases, other_tokens, own_tokens = stage(
        info, late[2:4], Features(late[0], late[1], chips), [(0, NEAR)], [(0, chips)]
    )
    for bit in range(bits - 1, 1, -1):
        arrived = [to_chip(dense[chain], 1 << bit) for chain in every]
        if bit == bits - 1:
            arrived[0], own_tokens, other_tokens, *bases = lax.optimization_barrier(
                (arrived[0], own_tokens, other_tokens, *bases)
            )
        for chain in every:
            if chain:
                (arrived[chain],) = after((arrived[chain],), dense[chain - 1])
            dense[chain] = dense[chain] + arrived[chain]
    total = None
    for chain in every:
        own = near_pieces(dense[chain])
        if chain:
            own[1:3] = after(own[1:3], first)
            (own[3],) = after((own[3],), total)
        first = own[1]
        total = rotate(info, chain, own, [to_core(value) for value in own], bases, total)

    partial, first, second = total

    def number(p, i, q, j):
        return p * count + i, q * count + j

    meet = [number(p, i, *((p, i ^ 1) if i % 2 == p else (1 - p, i))) for p in range(2) for i in range(count)]
    cross = [number(p, i, 1 - p, i ^ 1) for p in range(2) for i in range(count) if i % 2 != p]
    met, crossed = lax.ppermute(first, EVERYONE, meet), lax.ppermute(second, EVERYONE, cross)
    piece = meet_halves(info, partial, met, crossed)

    held = [piece[None]]
    for bit in range(2, bits):
        held.append(to_chip(held[0] if len(held) == 1 else jnp.concatenate(held, axis=0), 1 << bit))
    arrays, own, sib = [], [], []
    for num, source in enumerate(held):
        if num == 1:
            given_away, source = lax.optimization_barrier((given_away, source))
        low, high = near_gather(source)
        if num == 0:
            crossing = [lax.ppermute(value, EVERYONE, across) for value in (low, high)]
        entries = source.shape[0]
        for step in range(NEAR):
            for places, at, base in ((own, step, 0), (sib, SIBLING[step], 2)):
                places += [(4 * num + base + at // 2, at % 2 * entries + entry) for entry in range(entries)]
        sib_high = to_core(high)
        if num == 1:
            early_sib = to_core(crossing[0])
            sib_high, early_sib, *crossing = lax.optimization_barrier((sib_high, early_sib, *crossing))
        arrays += [low, high, to_core(low), sib_high]

    wide_in = basis_in.shape[0]
    theirs = project(arrays, own[NEAR:], sib[NEAR:], wide_in, [given_away], [(0, chips - NEAR)], jnp.bfloat16)
    back = lax.ppermute(jnp.stack(theirs), EVERYONE, across)
    for places, base in ((own, 0), (sib, 2)):
        places += [(len(arrays) + number, place) for number, place in places[:NEAR]]
    late = after(crossing[1:], theirs[0])
    arrays += crossing + [early_sib] + [to_core(value) for value in late]
    kept = [(0, chips), (chips, chips + NEAR)]
    mine = project(arrays, own, sib, wide_in, [own_tokens, other_tokens], kept, jnp.float32)

    held = score(more, count, mine, back, num_queries, rank_count)
    for bit in range(bits + 1):
        held = held + lax.ppermute(held, "blk", [(i, i ^ (1 << bit)) for i in range(count)])
    return own_sequence(more, count, held, num_queries)


def solution(mesh):
    placed = (
        P(("parts", "blk"), None, None),
        P(("parts", "blk"), None, None),
        P("blk", None),
        P("blk", None),
        P("blk", None, None),
        P("blk", None, None),
        P(),
        P("parts"),
        P("parts"),
    )
    return jax.shard_map(
        shards, mesh=mesh, in_specs=placed, out_specs=P(("parts", "blk"), None), check_vma=False
    )
```

```python
import jax
import jax.numpy as jnp
from jax import lax
from jax.experimental import pallas as pl
from jax.experimental.pallas import tpu as pltpu
from jax.sharding import PartitionSpec as P

ROWS = (((1,), (1,)), ((), ()))
EVERYONE = ("parts", "blk")
NEAR = 4
CHAINS = 2
PART, CORE, CHIP, ME, NEAR_AT, CHIP_AT = 0, 1, 2, 3, 4, 8
MIB = 1024 * 1024


def dot_rows(left, right):
    return lax.dot_general(left, right, ROWS, preferred_element_type=jnp.float32)


NEAR_MASKS = ((0, 1, 2, 3), (0, 2, 1, 3))
SIBLING = (0, 2, 1, 3)


def after(values, other):
    return list(lax.optimization_barrier((*values, other)))[:-1]


VMEM = pl.BlockSpec(memory_space=pltpu.VMEM)
SMEM = pl.BlockSpec(memory_space=pltpu.SMEM)
HBM = pl.BlockSpec(memory_space=pltpu.HBM)


def in_hbm(value):
    return pltpu.with_memory_space_constraint(value, pltpu.HBM)


def in_vmem(value):
    return pltpu.with_memory_space_constraint(value, pltpu.VMEM)


def lanes_at(number, width):
    return pl.ds(pl.multiple_of(number * width, 128), width)


def copy_all(copies):
    for copy in copies:
        copy.start()
    for copy in copies:
        copy.wait()


def estimate(flops, moved):
    return pl.CostEstimate(flops=flops, bytes_accessed=moved, transcendentals=0)


class Features:
    def __init__(self, acts, grads, chips):
        self.tokens, self.chips, self.kind = acts.shape[0], chips, acts.dtype
        self.acts, self.grads = acts, grads
        self.wide_in, self.wide_out = acts.shape[1] // 2 // chips, grads.shape[1] // 2 // chips
        self.wide = self.wide_in + self.wide_out
        self.aligned = not (self.wide_in % 128 or self.wide_out % 128)

    def shapes(self, ranges):
        return [pltpu.VMEM((self.tokens, (end - begin) * self.wide), self.kind) for begin, end in ranges]

    def copies(self, sources, outs, ranges, plane, chip_at, sems):
        result = []
        for out, (first, last) in zip(outs, ranges):
            for spot in range(first, last):
                number = 2 * chip_at(spot) + plane
                for source, width, begin in zip(sources, (self.wide_in, self.wide_out), (0, self.wide_in)):
                    result.append(
                        pltpu.make_async_copy(
                            source.at[:, lanes_at(number, width)],
                            out.at[:, pl.ds((spot - first) * self.wide + begin, width)],
                            sems.at[len(result)],
                        )
                    )
        return result

    def plain(self, ranges, plane, chip_at):
        some = [
            jnp.take(jnp.take(value.reshape(self.tokens, self.chips, 2, width), plane, axis=2), chip_at, axis=1)
            for value, width in ((self.acts, self.wide_in), (self.grads, self.wide_out))
        ]
        some = jnp.concatenate(some, axis=2)
        return [some[:, begin:end].reshape(self.tokens, -1) for begin, end in ranges]


def rank_halves(info, left, right):
    half_rank = left.shape[1] // 2
    widths = [factor.shape[2] // (2 * CHAINS * NEAR) for factor in (left, right)]
    wide = sum(widths)

    def kernel(where, left, right, away, kept, sems):
        copies = []
        for side, out in enumerate((away, kept)):
            half = where[CORE] if side else 1 - where[CORE]
            rows = pl.ds(pl.multiple_of(half * half_rank, half_rank), half_rank)
            for chunk in range(NEAR):
                for chain in range(CHAINS):
                    number = (where[PART] * CHAINS + chain) * NEAR + chunk
                    for source, width, begin in zip((left, right), widths, (0, widths[0])):
                        copies.append(
                            pltpu.make_async_copy(
                                source.at[0, rows, lanes_at(number, width)],
                                out.at[chunk, chain, :, pl.ds(begin, width)],
                                sems.at[len(copies)],
                            )
                        )
        copy_all(copies)

    shape = (NEAR, CHAINS, half_rank, wide)
    return pl.pallas_call(
        kernel,
        in_specs=[SMEM] + [HBM] * 2,
        out_specs=[VMEM] * 2,
        out_shape=[pltpu.VMEM(shape, left.dtype)] * 2,
        scratch_shapes=[pltpu.SemaphoreType.DMA((4 * NEAR * CHAINS,))],
        compiler_params=pltpu.CompilerParams(vmem_limit_bytes=4 * MIB),
        cost_estimate=estimate(0, 8 * NEAR * CHAINS * half_rank * wide),
        name="rank_halves",
    )(info, in_hbm(left), in_hbm(right))


def messages_of(info, kept, received):
    def kernel(where, kept, received, *outs):
        for mask, out in enumerate(outs):
            chunk = (where[CHIP] % NEAR) ^ mask
            out[0] = kept[chunk]
            out[1] = received[chunk]

    shape = jax.ShapeDtypeStruct((2,) + kept.shape[1:], kept.dtype)
    return pl.pallas_call(
        kernel,
        in_specs=[SMEM, VMEM, VMEM],
        out_specs=[VMEM] * NEAR,
        out_shape=[shape] * NEAR,
        compiler_params=pltpu.CompilerParams(vmem_limit_bytes=4 * MIB),
        cost_estimate=estimate(0, 4 * 2 * kept.size),
        name="messages",
    )(info, kept, received)


def stage(info, bases, features, given, kept):
    shapes = [(basis.shape[0], basis.shape[1] // 2) for basis in bases]
    ranges = given + kept if features.aligned else []
    total = sum(end - begin for begin, end in ranges)
    plain = []
    if not features.aligned:
        chip_at = info[CHIP_AT : CHIP_AT + features.chips]
        plain = features.plain(given, 1 - info[PART], chip_at) + features.plain(kept, info[PART], chip_at)
        if not bases:
            return plain

    def kernel(where, acts, grads, *rest):
        sources, outs, (sems, more) = rest[: len(bases)], rest[len(bases) : -2], rest[-2:]
        copies = []
        moved = 0
        for num, out in enumerate(outs[len(bases) :]):
            plane = 1 - where[PART] if num < len(given) else where[PART]
            count = 2 * (ranges[num][1] - ranges[num][0])
            copies += features.copies(
                (acts, grads),
                [out],
                ranges[num : num + 1],
                plane,
                lambda spot: where[CHIP_AT + spot],
                more.at[pl.ds(moved, count)],
            )
            moved += count
        for num, (basis, shape) in enumerate(zip(sources, shapes)):
            copies.append(pltpu.make_async_copy(basis.at[:, lanes_at(where[PART], shape[1])], outs[num], sems.at[num]))
        copy_all(copies)

    results = pl.pallas_call(
        kernel,
        in_specs=[SMEM] + [HBM] * (2 + len(bases)),
        out_specs=[VMEM] * (len(bases) + len(ranges)),
        out_shape=[pltpu.VMEM(shape, features.kind) for shape in shapes] + features.shapes(ranges),
        scratch_shapes=[pltpu.SemaphoreType.DMA((2,)), pltpu.SemaphoreType.DMA((max(2 * total, 1),))],
        compiler_params=pltpu.CompilerParams(vmem_limit_bytes=4 * MIB),
        cost_estimate=estimate(0, 2 * sum(shape[0] * shape[1] for shape in shapes)),
        name="stage",
    )(info, *map(in_hbm, (features.acts, features.grads, *bases)))
    return list(results) + plain


def choose(info, queries, found):
    ranks, wide = found[0].shape[2:]
    chips = (info.shape[0] - CHIP_AT - queries) // 5

    def kernel(where, *rest):
        outs = rest[NEAR:]
        for query in range(queries):
            owner = where[CHIP_AT + chips + query]
            place = pl.ds(query * ranks, ranks)
            mask_of = (owner // 2) ^ where[CHIP]
            side = (owner % 2) ^ where[CORE]
            for chain, out in enumerate(outs):
                for mask in range(NEAR):

                    @pl.when(mask_of == mask)
                    def _():
                        out[place] = rest[mask][side, chain]

                @pl.when(mask_of >= NEAR)
                def _():
                    out[place] = jnp.zeros((ranks, wide), out.dtype)

    return pl.pallas_call(
        kernel,
        in_specs=[SMEM] + [VMEM] * NEAR,
        out_specs=[VMEM] * CHAINS,
        out_shape=[jax.ShapeDtypeStruct((queries * ranks, wide), found[0].dtype)] * CHAINS,
        compiler_params=pltpu.CompilerParams(vmem_limit_bytes=4 * MIB),
        cost_estimate=estimate(0, 4 * queries * ranks * wide * CHAINS),
        name="choose",
    )(info, *found)


def meet_halves(info, partial, met, crossed):
    def kernel(where, partial, met, crossed, out):
        @pl.when(where[CORE] == where[PART])
        def _():
            out[...] = (partial[...] + met[...].astype(jnp.float32)).astype(out.dtype)

        @pl.when(where[CORE] != where[PART])
        def _():
            out[...] = (crossed[...].astype(jnp.float32) + met[...].astype(jnp.float32)).astype(out.dtype)

    return pl.pallas_call(
        kernel,
        in_specs=[SMEM] + [VMEM] * 3,
        out_specs=VMEM,
        out_shape=jax.ShapeDtypeStruct(met.shape, met.dtype),
        compiler_params=pltpu.CompilerParams(vmem_limit_bytes=4 * MIB),
        cost_estimate=estimate(2 * partial.size, 10 * partial.size),
        name="meet_halves",
    )(info, partial, met, crossed)


def rotate(info, chain, own, sib, bases, total):
    last = chain == CHAINS - 1
    ranks, wide = own[0].shape
    wide_in = bases[0].shape[1] // (CHAINS * NEAR)
    widths = (wide_in, wide - wide_in)
    rows_in = bases[0].shape[0]
    height = rows_in + bases[1].shape[0]
    spans = ((0, rows_in, 0, wide_in), (rows_in, height, wide_in, wide))

    def kernel(where, *rest):
        own_here, sib_here, bases_here, rest = rest[:NEAR], rest[NEAR : 2 * NEAR], rest[2 * NEAR :][:2], rest[2 * NEAR + 2 :]
        if total is not None:
            start, rest = rest[0], rest[1:]
        outs, acc = rest[:-1], rest[-1]
        for spot in range(NEAR):
            factor = jnp.concatenate([own_here[spot][...], sib_here[SIBLING[spot]][...]], axis=0)
            for num, (from_row, to_row, from_lane, to_lane) in enumerate(spans):
                block = bases_here[num][:, lanes_at(chain * NEAR + where[NEAR_AT + spot], widths[num])]
                value = dot_rows(block, factor[:, from_lane:to_lane])
                if spot:
                    value = value + acc[from_row:to_row]
                elif total is not None:
                    value = value + start[from_row:to_row]
                acc[from_row:to_row] = value
        if last:
            value = acc[...].T
            outs[0][...] = value[:ranks]
            outs[1][...] = jnp.where(where[CORE] == where[PART], value[ranks:], value[:ranks]).astype(jnp.bfloat16)
            outs[2][...] = value[ranks:].astype(jnp.bfloat16)
        else:
            outs[0][...] = acc[...]

    if last:
        shapes = [jax.ShapeDtypeStruct((ranks, height), kind) for kind in (jnp.float32, jnp.bfloat16, jnp.bfloat16)]
    else:
        shapes = [jax.ShapeDtypeStruct((height, 2 * ranks), jnp.float32)]
    given = [] if total is None else [total]
    moved = sum((to_row - from_row) * (to_lane - from_lane) for from_row, to_row, from_lane, to_lane in spans)
    results = pl.pallas_call(
        kernel,
        in_specs=[SMEM] + [VMEM] * (2 * NEAR + 2 + len(given)),
        out_specs=[VMEM] * len(shapes),
        out_shape=shapes,
        scratch_shapes=[pltpu.VMEM((height, 2 * ranks), jnp.float32)],
        compiler_params=pltpu.CompilerParams(vmem_limit_bytes=4 * MIB),
        cost_estimate=estimate(4 * ranks * NEAR * moved, 2 * NEAR * moved),
        name="rotate",
    )(info, *own, *sib, *map(in_vmem, bases), *given)
    return tuple(results) if last else results[0]


def project(arrays, own, sib, wide_in, tokens_in, pieces, kind):
    chips = len(own)
    ranks, wide = arrays[0].shape[1:]
    tokens = tokens_in[0].shape[0]
    if wide_in % 128 or wide % 128:
        both = jnp.stack([jnp.concatenate([arrays[i][m], arrays[j][n]], axis=0) for (i, m), (j, n) in zip(own, sib)])
        held = jnp.concatenate(tokens_in, axis=1).reshape(tokens, chips, wide)
        return [
            jnp.einsum("tgf,gcf->tc", held[:, :, lanes], both[:, :, lanes], preferred_element_type=jnp.float32).astype(
                kind
            )
            for lanes in (slice(0, wide_in), slice(wide_in, wide))
        ]

    def kernel(*rest):
        factors, rest = rest[: len(arrays)], rest[len(arrays) :]
        held, rest = rest[: len(tokens_in)], rest[len(tokens_in) :]
        outs, acc = rest[:2], rest[2]
        for source, (first, last) in zip(held, pieces):
            for spot in range(first, last):
                (i, m), (j, n) = own[spot], sib[spot]
                factor = jnp.concatenate([factors[i][m], factors[j][n]], axis=0)
                for num, (begin, end) in enumerate(((0, wide_in), (wide_in, wide))):
                    base = (spot - first) * wide
                    value = dot_rows(source[:, base + begin : base + end], factor[:, begin:end])
                    acc[num] = value if spot == 0 else acc[num] + value
        for num, out in enumerate(outs):
            out[...] = acc[num].astype(kind)

    return pl.pallas_call(
        kernel,
        in_specs=[VMEM] * (len(arrays) + len(tokens_in)),
        out_specs=[VMEM] * 2,
        out_shape=[jax.ShapeDtypeStruct((tokens, 2 * ranks), kind)] * 2,
        scratch_shapes=[pltpu.VMEM((2, tokens, 2 * ranks), jnp.float32)],
        compiler_params=pltpu.CompilerParams(vmem_limit_bytes=4 * MIB),
        cost_estimate=estimate(4 * tokens * ranks * chips * wide, 4 * ranks * chips * wide),
        name="project",
    )(*arrays, *map(in_vmem, tokens_in))


def score(info, slots, mine, back, queries, rank_count):
    tokens, columns = mine[0].shape
    half_rank = rank_count // 2
    lanes = -(-slots * queries // 128) * 128
    lengths_at = info.shape[0] - 2 * slots

    def kernel(where, mine_in, mine_out, back, out):
        sequence = where[lengths_at + slots + where[ME]]
        live = lax.broadcasted_iota(jnp.int32, (tokens, columns), 0) < where[lengths_at + sequence]
        products = (mine_in[...] + back[0].astype(jnp.float32)) * (mine_out[...] + back[1].astype(jnp.float32))
        sums = jnp.sum(jnp.where(live, products, 0.0), axis=0, keepdims=True)
        query_of = lax.broadcasted_iota(jnp.int32, (1, columns), 1) % (queries * half_rank) // half_rank
        lane = lax.broadcasted_iota(jnp.int32, (1, lanes), 1)
        row = jnp.zeros((1, lanes), jnp.float32)
        for query in range(queries):
            value = jnp.sum(jnp.where(query_of == query, sums, 0.0), axis=1, keepdims=True) / rank_count
            row = jnp.where(lane == sequence * queries + query, value, row)
        out[...] = row

    return pl.pallas_call(
        kernel,
        in_specs=[SMEM] + [VMEM] * 3,
        out_specs=VMEM,
        out_shape=jax.ShapeDtypeStruct((1, lanes), jnp.float32),
        compiler_params=pltpu.CompilerParams(vmem_limit_bytes=4 * MIB),
        cost_estimate=estimate(6 * tokens * columns, 12 * tokens * columns),
        name="score",
    )(info, *mine, back)


def own_sequence(info, held, queries):

    lanes = held.shape[1]

    def kernel(where, held, out):
        out[...] = pltpu.roll(held[...], lanes - where[ME] * queries, 1)[:, :queries]

    return pl.pallas_call(
        kernel,
        in_specs=[SMEM, VMEM],
        out_specs=VMEM,
        out_shape=jax.ShapeDtypeStruct((1, queries), jnp.float32),
        compiler_params=pltpu.CompilerParams(vmem_limit_bytes=4 * MIB),
        cost_estimate=estimate(0, 4 * held.size),
        name="own_sequence",
    )(info, held)


def shards(
    activations,
    output_grads,
    basis_in,
    basis_out,
    query_left,
    query_right,
    owners,
    lengths,
    slot_plan,
):
    count = lax.axis_size("blk")
    chips = count // 2
    bits = chips.bit_length() - 1
    me = lax.axis_index("blk")
    part = lax.axis_index("parts")
    core, chip = me % 2, me // 2
    seqs_here, max_length, width_in = activations.shape
    num_queries = owners.shape[0]
    rank_count = query_left.shape[1]
    half_rank = rank_count // 2
    ranks = num_queries * half_rank
    tokens = seqs_here * max_length
    acts = activations.reshape(tokens, width_in)
    grads = output_grads.reshape(tokens, -1)
    across = [(p * count + i, (1 - p) * count + i) for p in range(2) for i in range(count)]

    def to_chip(value, mask):
        return lax.ppermute(value, "blk", [(i, i ^ (2 * mask)) for i in range(count)])

    def along(value, first, second):
        return lax.ppermute(value, "blk", [(i, i ^ (2 << (second if i % 2 else first))) for i in range(count)])

    def to_core(value):
        return lax.ppermute(value, "blk", [(i, i ^ 1) for i in range(count)])

    def near_gather(value, before=None):
        first = along(value, 0, 1)
        if before is not None:
            (first,) = after((first,), before)
        low = jnp.concatenate([value, first], axis=0)
        return low, along(low, 1, 0)

    def near_pieces(value):
        first = along(value, 0, 1)
        second = along(value, 1, 0)
        return [value, first, second, along(first, 1, 0)]

    near_at = jnp.where(core == 0, jnp.array(NEAR_MASKS[0], jnp.int32), jnp.array(NEAR_MASKS[1], jnp.int32)) ^ (
        chip % NEAR
    )
    sources = [[0]]
    for bit in range(2, bits):
        sources.append([mask | (1 << bit) for group in sources for mask in group])
    orders = [[far | near for group in sources for near in NEAR_MASKS[side] for far in group] for side in range(2)]
    chip_at = jnp.where(core == 0, jnp.array(orders[0], jnp.int32), jnp.array(orders[1], jnp.int32)) ^ chip

    (info,) = lax.optimization_barrier((jnp.concatenate([jnp.stack([part, core, chip, me]), near_at, chip_at]),))

    far = (NEAR, chips)

    away, kept = rank_halves(info, query_left, query_right)
    more = jnp.concatenate([info, *after((owners, lengths, slot_plan), away)])
    received, more = lax.optimization_barrier((to_core(away), more))
    messages = messages_of(info, kept, received)

    every = range(CHAINS)
    found = [to_chip(value, mask) if mask else value for mask, value in enumerate(messages)]
    dense = list(choose(more, num_queries, found))
    early = Features(*after((acts, grads), messages[0]), chips)
    (given_away,) = stage(info, [], early, [far], [])
    late = lax.optimization_barrier((acts, grads, basis_in, basis_out, given_away))
    given_away = lax.ppermute(given_away, EVERYONE, across)
    bases = stage(info, late[2:4], Features(*late[:2], chips), [], [])
    for bit in range(bits - 1, 1, -1):
        arrived = [to_chip(dense[chain], 1 << bit) for chain in every]
        if bit == bits - 1:
            arrived[0], *bases = lax.optimization_barrier((arrived[0], *bases))
        for chain in every:
            if chain:
                (arrived[chain],) = after((arrived[chain],), dense[chain - 1])
            dense[chain] = dense[chain] + arrived[chain]
    total = None
    for chain in every:
        own = near_pieces(dense[chain])
        if chain:
            own[1:3] = after(own[1:3], first)
            (own[3],) = after((own[3],), total)
        first = own[1]
        total = rotate(info, chain, own, [to_core(value) for value in own], bases, total)

    partial, first, second = total

    def number(p, i, q, j):
        return p * count + i, q * count + j

    meet = [number(p, i, *((p, i ^ 1) if i % 2 == p else (1 - p, i))) for p in range(2) for i in range(count)]
    cross = [number(p, i, 1 - p, i ^ 1) for p in range(2) for i in range(count) if i % 2 != p]
    met, crossed = lax.ppermute(first, EVERYONE, meet), lax.ppermute(second, EVERYONE, cross)
    late = Features(*after((acts, grads), first), chips)
    other_tokens, own_tokens = stage(info, [], late, [(0, NEAR)], [(0, chips)])
    met, other_tokens, own_tokens = lax.optimization_barrier((met, other_tokens, own_tokens))
    piece = meet_halves(info, partial, met, crossed)

    held = [piece[None]]
    for bit in range(2, bits):
        held.append(to_chip(held[0] if len(held) == 1 else jnp.concatenate(held, axis=0), 1 << bit))
    arrays, own, sib = [], [], []
    for num, source in enumerate(held):
        if num == 1:
            given_away, source = lax.optimization_barrier((given_away, source))
        low, high = near_gather(source)
        if num == 0:
            crossing = [lax.ppermute(value, EVERYONE, across) for value in (low, high)]
        entries = source.shape[0]
        for step in range(NEAR):
            for places, at, base in ((own, step, 0), (sib, SIBLING[step], 2)):
                places += [(4 * num + base + at // 2, at % 2 * entries + entry) for entry in range(entries)]
        sib_high = to_core(high)
        if num == 1:
            early_sib = to_core(crossing[0])
            sib_high, early_sib, *crossing = lax.optimization_barrier((sib_high, early_sib, *crossing))
        arrays += [low, high, to_core(low), sib_high]

    wide_in = basis_in.shape[0]
    theirs = project(arrays, own[NEAR:], sib[NEAR:], wide_in, [given_away], [(0, chips - NEAR)], jnp.bfloat16)
    back = lax.ppermute(jnp.stack(theirs), EVERYONE, across)
    for places, base in ((own, 0), (sib, 2)):
        places += [(len(arrays) + number, place) for number, place in places[:NEAR]]
    late = after(crossing[1:], theirs[0])
    arrays += crossing + [early_sib] + [to_core(value) for value in late]
    kept = [(0, chips), (chips, chips + NEAR)]
    mine = project(arrays, own, sib, wide_in, [own_tokens, other_tokens], kept, jnp.float32)

    held = score(more, count, mine, back, num_queries, rank_count)
    for bit in range(bits + 1):
        held = held + lax.ppermute(held, "blk", [(i, i ^ (1 << bit)) for i in range(count)])
    return own_sequence(info, held, num_queries)


def solution(mesh):
    placed = (
        P(("parts", "blk"), None, None),
        P(("parts", "blk"), None, None),
        P("blk", None),
        P("blk", None),
        P("blk", None, None),
        P("blk", None, None),
        P(),
        P("parts"),
        P("parts"),
    )
    return jax.shard_map(
        shards, mesh=mesh, in_specs=placed, out_specs=P(("parts", "blk"), None), check_vma=False
    )
```
